256 devices in a mesh: dp: 16 (over x, z_lo, core), tensor: 16 (over z_hi, y).
Axes of the slice: x: 4, y: 4, z: 8 (z_hi: 4, z_lo: 2; z = z_hi * 2 + z_lo), core: 2. Of those that a mesh axis runs over, the one named last changes fastest.
Arguments:
- tokens_in: bfloat16 [6144, 8192], P('dp', 'tensor'), may hold values from -21 to 21
- out_grad: bfloat16 [6144, 8192], P('dp', 'tensor'), may hold values from -6 to 6
- q_weight: bfloat16 [8192, 8192], P('dp', 'tensor'), may hold values from -0.0625 to 0.0625
- kv_weight: bfloat16 [8192, 2048], P('dp', 'tensor'), may hold values from -0.0625 to 0.0625
Outputs:
- input_grad: bfloat16 [6144, 8192], P('dp', 'tensor')
- q_grad: bfloat16 [8192, 8192], P('dp', 'tensor')
- kv_grad: bfloat16 [8192, 2048], P('dp', 'tensor')
The draws below stay inside these ranges and needn't reach their ends.
All inputs are finite; a program needn't handle non-finite values.
Results may differ from the reference program's by a relative error of at most 0.025.
Values may be sent and summed in bfloat16 or wider, within the bound.
A program may use at most 128 MiB of HBM per device.

```python
import math
import jax
import jax.numpy as jnp
from jax import lax

D = 8192
HD = 128
HEADS_DEV = 4
TOK_DEV = 384
HEADS = 64
KV_HEADS = 8
TOKENS = 6144
N_DP = 16
N_TENSOR = 16


def draw_tokens_in(key, part):
    key = jax.random.fold_in(key, 11)
    key_base, key_scale = jax.random.split(key)
    base = jnp.clip(jax.random.normal(key_base, (TOKENS, D), jnp.float32), -5.0, 5.0)
    scale = jnp.exp(jax.random.uniform(key_scale, (TOKENS, 1), jnp.float32, 0.0, math.log(3.0)))
    return (base * scale).astype(jnp.bfloat16)


def block_levels(own_key, extent, cuts, smallest, high):
    gain = 1.0
    for position, parts in cuts:
        steps = jax.random.uniform(jax.random.fold_in(jax.random.fold_in(own_key, 6), position), (parts,), jnp.float32, smallest / len(cuts), high / len(cuts))
        gain = gain * jnp.repeat(jnp.exp(steps), extent[position] // parts).reshape((-1,) + (1,) * (len(extent) - 1 - position))
    return gain


def noise(stream_key, extent, deviation, reach, cuts=(), kind=jnp.bfloat16):
    loudness = block_levels(stream_key, extent, cuts, -0.22, 0.18) if cuts else 1.0
    array = jax.random.normal(stream_key, extent, jnp.float32) * deviation * loudness
    return jnp.minimum(jnp.maximum(array, -reach), reach).astype(kind)


def setup_inputs(seed: int = 0) -> dict:
    streams_of = jax.random.split(jax.random.key(seed), 5)
    return {
        "tokens_in": draw_tokens_in(jax.random.fold_in(streams_of[4], 71), 0),
        "out_grad": noise(streams_of[1], (TOKENS, HEADS * HD), 1.0, 6.0, ((0, 16), (1, 16))),
        "q_weight": noise(streams_of[2], (D, HEADS * HD), D ** -0.5, 0.0625, ((0, 16), (1, 16))),
        "kv_weight": noise(streams_of[3], (D, 2 * KV_HEADS * HD), D ** -0.5, 0.0625, ((0, 16), (1, 16))),
    }


def rope_tables(length, size):
    half = size // 2
    positions = jnp.arange(length, dtype=jnp.float32)
    inverse = 500000.0 ** (-(jnp.arange(half, dtype=jnp.float32) * 2.0 / size))
    angle = positions[:, None] * inverse[None, :]
    return jnp.cos(angle), jnp.sin(angle)


def rotate(value, cosine, sine):
    half = value.shape[-1] // 2
    first = value[..., :half]
    second = value[..., half:]
    return jnp.concatenate([first * cosine - second * sine, second * cosine + first * sine], axis=-1)


def group_backward(x_rows, grad_rows, wq_wide, wkv_wide, q_weight, kv_weight):
    length = x_rows.shape[0]
    scale = HD ** -0.5
    cosine, sine = rope_tables(length, HD)
    cos_h = cosine[:, None, :]
    sin_h = sine[:, None, :]
    q_proj = jnp.dot(x_rows, q_weight, preferred_element_type=jnp.float32).reshape(length, HEADS, HD)
    queries = rotate(q_proj, cos_h, sin_h).astype(jnp.bfloat16)
    kv_proj = jnp.dot(x_rows, kv_weight, preferred_element_type=jnp.float32).reshape(length, KV_HEADS, 2, HD)
    keys = rotate(kv_proj[:, :, 0], cos_h, sin_h).astype(jnp.bfloat16)
    values = kv_proj[:, :, 1].astype(jnp.bfloat16)
    group = HEADS // KV_HEADS
    keys_wide = jnp.repeat(keys.astype(jnp.float32), group, axis=1)
    values_wide = jnp.repeat(values.astype(jnp.float32), group, axis=1)
    q_float = queries.astype(jnp.float32)
    scores = jnp.einsum("shd,thd->hst", q_float, keys_wide) * scale
    causal = jnp.arange(length)[None, :] <= jnp.arange(length)[:, None]
    scores = jnp.where(causal[None], scores, -jnp.inf)
    top = jnp.max(scores, axis=-1, keepdims=True)
    expo = jnp.exp(scores - top)
    probs = expo / jnp.sum(expo, axis=-1, keepdims=True)
    probs_low = lax.optimization_barrier(probs.astype(jnp.bfloat16)).astype(jnp.float32)
    grad_float = grad_rows.reshape(length, HEADS, HD).astype(jnp.float32)
    dprobs = jnp.einsum("shd,thd->hst", grad_float, values_wide)
    delta = jnp.sum(probs * dprobs, axis=-1, keepdims=True)
    dscores = lax.optimization_barrier((probs * (dprobs - delta) * scale).astype(jnp.bfloat16)).astype(jnp.float32)
    dq = jnp.einsum("hst,thd->shd", dscores, keys_wide)
    dq = rotate(dq, cos_h, -sin_h).astype(jnp.bfloat16).reshape(length, HEADS * HD)
    dk_heads = jnp.einsum("hst,shd->thd", dscores, q_float)
    dv_heads = jnp.einsum("hst,shd->thd", probs_low, grad_float)
    key_sum = jnp.sum(dk_heads.reshape(length, KV_HEADS, group, HD), axis=2)
    value_sum = jnp.sum(dv_heads.reshape(length, KV_HEADS, group, HD), axis=2)
    key_grad = rotate(key_sum, cos_h, -sin_h).astype(jnp.bfloat16)
    value_grad = value_sum.astype(jnp.bfloat16)
    roles = jnp.stack([key_grad, value_grad], axis=2).reshape(length, 2 * KV_HEADS * HD)
    dq_dev = dq.reshape(length, N_TENSOR, HEADS_DEV * HD).astype(jnp.float32)
    roles_dev = roles.reshape(length, N_TENSOR, HD).astype(jnp.float32)
    terms = jnp.einsum("stc,dtc->tsd", dq_dev, wq_wide) + jnp.einsum("stc,dtc->tsd", roles_dev, wkv_wide)
    terms = lax.optimization_barrier(terms.astype(jnp.bfloat16)).astype(jnp.float32)
    input_rows = jnp.sum(terms, axis=0).astype(jnp.bfloat16)
    q_part = jnp.dot(x_rows.T, dq, preferred_element_type=jnp.float32).astype(jnp.bfloat16)
    kv_part = jnp.dot(x_rows.T, roles, preferred_element_type=jnp.float32).astype(jnp.bfloat16)
    return input_rows, q_part, kv_part


def reference(tokens_in, out_grad, q_weight, kv_weight):
    x_groups = tokens_in.reshape(N_DP, TOK_DEV, D)
    grad_groups = out_grad.reshape(N_DP, TOK_DEV, HEADS * HD)
    wq_wide = q_weight.astype(jnp.float32).reshape(D, N_TENSOR, HEADS_DEV * HD)
    wkv_wide = kv_weight.astype(jnp.float32).reshape(D, N_TENSOR, HD)

    def step(carry, item):
        input_rows, q_part, kv_part = group_backward(item[0], item[1], wq_wide, wkv_wide, q_weight, kv_weight)
        return (carry[0] + q_part.astype(jnp.float32), carry[1] + kv_part.astype(jnp.float32)), input_rows

    start = (jnp.zeros((D, HEADS * HD), jnp.float32), jnp.zeros((D, 2 * KV_HEADS * HD), jnp.float32))
    sums, rows = lax.scan(step, start, (x_groups, grad_groups))
    return rows.reshape(TOKENS, D), sums[0].astype(jnp.bfloat16), sums[1].astype(jnp.bfloat16)
```

```python
import functools
import jax
import jax.numpy as jnp
import numpy as np
from jax import lax
from jax.sharding import PartitionSpec as P
from jax.experimental import pallas as pl
from jax.experimental.pallas import tpu as pltpu

MESH = pl.DeviceIdType.MESH
F32, BF16 = jnp.float32, jnp.bfloat16
TOK, FEAT, HD, HEADS, COLS = 384, 512, 128, 4, 640
HT, HW, HG = TOK // 2, FEAT // 2, COLS // 2
N_SEMS = 192


def rope_tables(length, size):
    half = size // 2
    positions = np.arange(length, dtype=np.float32)
    inverse = np.power(
        np.float32(500000.0), -(np.arange(half, dtype=np.float32) * np.float32(2.0) / np.float32(size))
    ).astype(np.float32)
    angle = (positions[:, None] * inverse[None, :]).astype(np.float32).astype(np.float64)
    cosine, sine = np.cos(angle), np.sin(angle)
    return (
        np.concatenate([cosine, cosine], axis=1).astype(np.float32),
        np.concatenate([-sine, sine], axis=1).astype(np.float32),
    )


def dot_nn(a, b):
    return lax.dot_general(a, b, (((1,), (0,)), ((), ())), preferred_element_type=F32)


def dot_nt(a, b):
    return lax.dot_general(a, b, (((1,), (1,)), ((), ())), preferred_element_type=F32)


def dot_tn(a, b):
    return lax.dot_general(a, b, (((0,), (0,)), ((), ())), preferred_element_type=F32)


def kernel(
    x_in, og_in, wq_in, wkv_in, cos_ref, sin_ref,
    dx_out, qg_out, kvg_out,
    xbuf, wbuf, xsib, og, acc, qbuf, kv, gbuf, gt, part, part_low, part_in,
    dxs, ry_full, ry_half, rz_full, rz_half,
    dws, rx_full, rx_half, rzl,
    local_sem, ss, rs,
):
    dp, tn = lax.axis_index("dp"), lax.axis_index("tensor")
    x, zl, c = dp // 4, (dp // 2) % 2, dp % 2
    zh, y = tn // 4, tn % 4
    role = y % 2
    is_key = role == 0

    def wb(dx, dz, dc):
        return ((x + dx) % 4) * 4 + ((zl + dz) % 2) * 2 + (c + dc) % 2

    def tb(dh, dy):
        return ((zh + dh) % 4) * 4 + (y + dy) % 4

    sib = (wb(0, 0, 1), tn)
    zlp = (wb(0, 1, 0), tn)
    xp, xm = (wb(1, 0, 0), tn), (wb(3, 0, 0), tn)
    yp, ym = (dp, tb(0, 1)), (dp, tb(0, 3))
    zp, zm = (dp, tb(1, 0)), (dp, tb(3, 0))
    mate = (dp, zh * 4 + y + 1 - 2 * role)

    names = {}
    pending = []

    def sem(name):
        return names.setdefault(name, len(names))

    def send(name, src, dst, to):
        k = sem(name)
        copy = pltpu.make_async_remote_copy(
            src_ref=src, dst_ref=dst, send_sem=ss.at[k], recv_sem=rs.at[k],
            device_id=to, device_id_type=MESH,
        )
        copy.start()
        pending.append(copy)

    def recv(name, dst):
        k = sem(name)
        pltpu.make_async_remote_copy(
            src_ref=dst, dst_ref=dst, send_sem=ss.at[k], recv_sem=rs.at[k],
            device_id=sib, device_id_type=MESH,
        ).wait_recv()

    def xs(block, h):
        return xbuf.at[block, pl.ds(h * HT, HT)]

    def ws(block, h):
        return wbuf.at[block, pl.ds(h * HW, HW)]

    own_x, own_w = tn, dp
    loads = [
        pltpu.make_async_copy(x_in, xbuf.at[own_x], local_sem.at[0]),
        pltpu.make_async_copy(wq_in, wbuf.at[own_w, :, pl.ds(0, FEAT)], local_sem.at[1]),
        pltpu.make_async_copy(wkv_in, wbuf.at[own_w, :, pl.ds(FEAT, HD)], local_sem.at[2]),
        pltpu.make_async_copy(og_in, og, local_sem.at[3]),
    ]
    for load in loads:
        load.start()
    barrier = pltpu.get_barrier_semaphore()
    neighbours = (sib, zlp, xp, xm, yp, ym, zp, zm)
    for to in neighbours:
        pl.semaphore_signal(barrier, inc=1, device_id=to, device_id_type=MESH)
    pl.semaphore_wait(barrier, len(neighbours))

    def send_x(name, block, h, to):
        send((name, h), xs(block, h), xs(block, h), to)

    def recv_x(name, block, h):
        recv((name, h), xs(block, h))

    def send_w(name, block, h, to):
        send((name, h), ws(block, h), ws(block, h), to)

    def recv_w(name, block, h):
        recv((name, h), ws(block, h))

    def spread_y(j, h):
        send_x(("yp", j), tb(j, 0), h, yp)
        send_x(("ym", j), tb(j, 0), h, ym)

    loads[0].wait()
    for h in (0, 1):
        send_x("zp", own_x, h, zp)
        send_x("zm", own_x, 1 - h, zm)
        send_x(("yp", 0), own_x, h, yp)
        send_x(("ym", 0), own_x, 1 - h, ym)
    loads[1].wait()
    loads[2].wait()
    for h in (0, 1):
        send_w(("xp", 0), own_w, h, xp)
        send_w(("xm", 0), own_w, 1 - h, xm)
    for h in (0, 1):
        send_w("sib", own_w, h, sib)

    def relay_y(j, which):
        if which == 0:
            recv_x(("yp", j), tb(j, 3), 0)
            send_x(("ypr", j), tb(j, 3), 0, yp)
        else:
            recv_x(("ym", j), tb(j, 1), 1)
            send_x(("ymr", j), tb(j, 1), 1, ym)

    def relay_x(dz, which):
        if which == 0:
            recv_w(("xp", dz), wb(3, dz, 0), 0)
            send_w(("xpr", dz), wb(3, dz, 0), 0, xp)
            send_w(("sxp", dz), wb(3, dz, 0), 0, sib)
        else:
            recv_w(("xm", dz), wb(1, dz, 0), 1)
            send_w(("xmr", dz), wb(1, dz, 0), 1, xm)
            send_w(("sxm", dz), wb(1, dz, 0), 1, sib)

    def rest_x(dz):
        recv_w(("xp", dz), wb(3, dz, 0), 1)
        send_w(("sxp", dz), wb(3, dz, 0), 1, sib)
        recv_w(("xm", dz), wb(1, dz, 0), 0)
        send_w(("sxm", dz), wb(1, dz, 0), 0, sib)

    def far_x(dz):
        recv_w(("xpr", dz), wb(2, dz, 0), 0)
        send_w(("sfar", dz), wb(2, dz, 0), 0, sib)
        recv_w(("xmr", dz), wb(2, dz, 0), 1)
        send_w(("sfar", dz), wb(2, dz, 0), 1, sib)

    def from_zl(h):
        block = wb(0, 1, 0)
        recv_w("zl", block, h)
        send_w(("xp", 1), block, h, xp)
        send_w(("xm", 1), block, h, xm)
        send_w("szl", block, h, sib)

    relay_y(0, 0)
    relay_y(0, 1)
    relay_x(0, 0)
    relay_x(0, 1)
    recv_x("zp", tb(3, 0), 0)
    spread_y(3, 0)
    recv_x("zm", tb(1, 0), 1)
    spread_y(1, 1)
    send_w("zl", own_w, 0, zlp)
    rest_x(0)
    relay_y(3, 0)
    relay_y(1, 1)
    recv_x("zp", tb(3, 0), 1)
    spread_y(3, 1)
    recv_x("zm", tb(1, 0), 0)
    spread_y(1, 0)
    send_w("zl", own_w, 1, zlp)
    send_x("zpr", tb(3, 0), 0, zp)
    send_x("zmr", tb(1, 0), 1, zm)
    far_x(0)
    from_zl(0)
    relay_y(3, 1)
    relay_y(1, 0)
    from_zl(1)
    recv_x("zpr", tb(2, 0), 0)
    spread_y(2, 0)
    recv_x("zmr", tb(2, 0), 1)
    spread_y(2, 1)
    relay_x(1, 0)
    relay_x(1, 1)
    relay_y(2, 0)
    relay_y(2, 1)
    rest_x(1)
    far_x(1)
    for j in (0, 3, 1, 2):
        recv_x(("yp", j), tb(j, 3), 1)
        recv_x(("ym", j), tb(j, 1), 0)
        recv_x(("ypr", j), tb(j, 2), 0)
        recv_x(("ymr", j), tb(j, 2), 1)
    for h in (0, 1):
        recv_w("sib", wb(0, 0, 1), h)
        recv_w("szl", wb(0, 1, 1), h)
        for dz in (0, 1):
            recv_w(("sxp", dz), wb(3, dz, 1), h)
            recv_w(("sxm", dz), wb(1, dz, 1), h)
            recv_w(("sfar", dz), wb(2, dz, 1), h)

    for i in range(8):
        send(("xsib", i), xbuf.at[2 * i + 1 - c], xsib.at[i], sib)

    acc[...] = dot_nn(xbuf[0], wbuf[0])

    def project(b, carry):
        acc[...] += dot_nn(xbuf[b], wbuf[b])
        return carry

    lax.fori_loop(1, 16, project, 0)

    def rot(u, rows=slice(None)):
        return u * cos_ref[rows, :] + pltpu.roll(u, HD // 2, 1) * sin_ref[rows, :]

    def unrot(u, rows=slice(None)):
        return u * cos_ref[rows, :] - pltpu.roll(u, HD // 2, 1) * sin_ref[rows, :]

    raw = acc[:, FEAT:COLS]
    kv[role] = jnp.where(is_key, rot(raw), raw).astype(BF16)
    send("kv", kv.at[role], kv.at[role], mate)
    for h in range(HEADS):
        qbuf[:, h * HD:(h + 1) * HD] = rot(acc[:, h * HD:(h + 1) * HD]).astype(BF16)
    part[...] = jnp.zeros_like(part)
    loads[3].wait()
    recv("kv", kv.at[1 - role])

    scale = HD ** -0.5

    def head(h, carry):
        cols = pl.ds(pl.multiple_of(h * HD, HD), HD)
        for i in range(TOK // HD):
            rows, n = slice(i * HD, (i + 1) * HD), (i + 1) * HD
            q, grad = qbuf[rows, cols], og[rows, cols]
            k, v = kv[0, :n], kv[1, :n]
            scores = dot_nt(q, k) * scale
            q_pos = lax.broadcasted_iota(jnp.int32, (HD, n), 0) + i * HD
            k_pos = lax.broadcasted_iota(jnp.int32, (HD, n), 1)
            scores = jnp.where(k_pos <= q_pos, scores, -jnp.inf)
            expo = jnp.exp(scores - jnp.max(scores, axis=-1, keepdims=True))
            probs = expo / jnp.sum(expo, axis=-1, keepdims=True)
            dprobs = dot_nt(grad, v)
            delta = jnp.sum(probs * dprobs, axis=-1, keepdims=True)
            dscores = (probs * (dprobs - delta) * scale).astype(BF16)
            dq = unrot(dot_nn(dscores, k), rows)
            gbuf[rows, cols] = dq.astype(BF16)
            gt[0, cols, rows] = dq.T.astype(BF16)
            part[0, :n] += dot_tn(dscores, q)
            part[1, :n] += dot_tn(probs.astype(BF16), grad)
        return carry

    lax.fori_loop(0, HEADS, head, 0)

    part_low[...] = part[1 - role].astype(BF16)
    send("part", part_low, part_in, mate)
    send("gt_q", gt.at[0, pl.ds(0, FEAT)], gt.at[1, pl.ds(0, FEAT)], sib)
    recv("part", part_in)
    total = part[role] + part_in[...].astype(F32)
    total = jnp.where(is_key, unrot(total), total)
    gbuf[:, FEAT:COLS] = total.astype(BF16)
    gt[0, FEAT:COLS, :] = total.T.astype(BF16)
    send("gt_kv", gt.at[0, pl.ds(FEAT, HD)], gt.at[1, pl.ds(FEAT, HD)], sib)
    for i in range(8):
        recv(("xsib", i), xsib.at[i])

    def dx_half(j, dy, h):
        return dot_nt(gbuf[h * HT:(h + 1) * HT, :], wbuf[tb(j, dy)])

    def dw_half(ddx, dz, h):
        b = wb(ddx, dz, 0)
        rows = slice(h * HG, (h + 1) * HG)
        return dot_nn(gt[0, rows, :], xbuf[b]) + dot_nn(gt[1, rows, :], xsib[b // 2])

    def tslot(ref, i, h):
        return ref.at[i, pl.ds(h * HT, HT)]

    def gslot(ref, i, h):
        return ref.at[i, pl.ds(h * HG, HG)]

    def load_t(ref, i, h):
        return ref[i, h * HT:(h + 1) * HT, :].astype(F32)

    def load_g(ref, i, h):
        return ref[i, h * HG:(h + 1) * HG, :].astype(F32)

    def put_dx(name, j, dy, h, value, dst, to):
        i = j * 4 + dy
        dxs[i, h * HT:(h + 1) * HT, :] = value.astype(BF16)
        send(name, tslot(dxs, i, h), dst, to)

    def put_dw(name, ddx, dz, h, value, dst, to):
        i = ddx * 2 + dz
        dws[i, h * HG:(h + 1) * HG, :] = value.astype(BF16)
        send(name, gslot(dws, i, h), dst, to)

    def s1(j):
        put_dx(("s1", j, 0), j, 2, 0, dx_half(j, 2, 0), ry_half.at[j * 2], yp)
        put_dx(("s1", j, 1), j, 2, 1, dx_half(j, 2, 1), ry_half.at[j * 2 + 1], ym)

    def s2n(j):
        put_dx(("s2", j, 0, 1), j, 1, 1, dx_half(j, 1, 1), tslot(ry_full, j * 2, 1), yp)
        put_dx(("s2", j, 1, 0), j, 3, 0, dx_half(j, 3, 0), tslot(ry_full, j * 2 + 1, 0), ym)

    def s2d(j):
        mine = dx_half(j, 1, 0)
        recv(("s1", j, 0), ry_half.at[j * 2])
        put_dx(("s2", j, 0, 0), j, 1, 0, mine + ry_half[j * 2].astype(F32), tslot(ry_full, j * 2, 0), yp)
        mine = dx_half(j, 3, 1)
        recv(("s1", j, 1), ry_half.at[j * 2 + 1])
        put_dx(
            ("s2", j, 1, 1), j, 3, 1, mine + ry_half[j * 2 + 1].astype(F32), tslot(ry_full, j * 2 + 1, 1), ym
        )

    def s3(j):
        for h in ((1, 0) if j == 1 else (0, 1)):
            mine = dx_half(j, 0, h)
            recv(("s2", j, 0, h), tslot(ry_full, j * 2, h))
            recv(("s2", j, 1, h), tslot(ry_full, j * 2 + 1, h))
            mine = mine + load_t(ry_full, j * 2, h) + load_t(ry_full, j * 2 + 1, h)
            if j == 2:
                put_dx(("z1", h), 2, 0, h, mine, rz_half.at[h], zp if h == 0 else zm)
            elif j == 0:
                recv(("z2", 0, h), tslot(rz_full, 0, h))
                recv(("z2", 1, h), tslot(rz_full, 1, h))
                mine = mine + load_t(rz_full, 0, h) + load_t(rz_full, 1, h)
                dx_out[h * HT:(h + 1) * HT, :] = mine.astype(BF16)
            else:
                side = 0 if j == 1 else 1
                if h == side:
                    recv(("z1", side), rz_half.at[side])
                    mine = mine + rz_half[side].astype(F32)
                put_dx(("z2", side, h), j, 0, h, mine, tslot(rz_full, side, h), zp if j == 1 else zm)

    def t1(dz):
        put_dw(("t1", dz, 0), 2, dz, 0, dw_half(2, dz, 0), rx_half.at[dz * 2], xp)
        put_dw(("t1", dz, 1), 2, dz, 1, dw_half(2, dz, 1), rx_half.at[dz * 2 + 1], xm)

    def t2n(dz):
        put_dw(("t2", dz, 0, 1), 1, dz, 1, dw_half(1, dz, 1), gslot(rx_full, dz * 2, 1), xp)
        put_dw(("t2", dz, 1, 0), 3, dz, 0, dw_half(3, dz, 0), gslot(rx_full, dz * 2 + 1, 0), xm)

    def t2d(dz):
        mine = dw_half(1, dz, 0)
        recv(("t1", dz, 0), rx_half.at[dz * 2])
        put_dw(("t2", dz, 0, 0), 1, dz, 0, mine + rx_half[dz * 2].astype(F32), gslot(rx_full, dz * 2, 0), xp)
        mine = dw_half(3, dz, 1)
        recv(("t1", dz, 1), rx_half.at[dz * 2 + 1])
        put_dw(
            ("t2", dz, 1, 1), 3, dz, 1, mine + rx_half[dz * 2 + 1].astype(F32), gslot(rx_full, dz * 2 + 1, 1), xm
        )

    def t3(dz):
        for h in (0, 1):
            mine = dw_half(0, dz, h)
            recv(("t2", dz, 0, h), gslot(rx_full, dz * 2, h))
            recv(("t2", dz, 1, h), gslot(rx_full, dz * 2 + 1, h))
            mine = mine + load_g(rx_full, dz * 2, h) + load_g(rx_full, dz * 2 + 1, h)
            if dz == 1:
                put_dw(("t3", h), 0, 1, h, mine, rzl.at[pl.ds(h * HG, HG)], zlp)
            else:
                recv(("t3", h), rzl.at[pl.ds(h * HG, HG)])
                mine = (mine + rzl[h * HG:(h + 1) * HG, :].astype(F32)).T.astype(BF16)
                if h == 0:
                    qg_out[:, :HG] = mine
                else:
                    qg_out[:, HG:] = mine[:, :FEAT - HG]
                    kvg_out[...] = mine[:, FEAT - HG:]

    s1(2)
    recv("gt_q", gt.at[1, pl.ds(0, FEAT)])
    recv("gt_kv", gt.at[1, pl.ds(FEAT, HD)])
    t1(1)
    s2n(2)
    s1(1)
    t2n(1)
    s2d(2)
    s2n(1)
    t1(0)
    s1(3)
    s3(2)
    s2d(1)
    t2d(1)
    s2n(3)
    s1(0)
    t2n(0)
    s3(1)
    s2d(3)
    t3(1)
    s2n(0)
    t2d(0)
    s3(3)
    s2d(0)
    t3(0)
    s3(0)

    for copy in pending:
        copy.wait_send()
    assert len(names) <= N_SEMS


def body(tokens_in, out_grad, q_weight, kv_weight):
    cosine, sine = rope_tables(TOK, HD)
    vmem = pl.BlockSpec(memory_space=pltpu.VMEM)
    anywhere = pl.BlockSpec(memory_space=pl.ANY)
    return pl.pallas_call(
        kernel,
        out_shape=(
            jax.ShapeDtypeStruct((TOK, FEAT), BF16),
            jax.ShapeDtypeStruct((FEAT, FEAT), BF16),
            jax.ShapeDtypeStruct((FEAT, HD), BF16),
        ),
        in_specs=[anywhere] * 4 + [vmem] * 2,
        out_specs=(vmem, vmem, vmem),
        scratch_shapes=[
            pltpu.VMEM((16, TOK, FEAT), BF16),
            pltpu.VMEM((16, FEAT, COLS), BF16),
            pltpu.VMEM((8, TOK, FEAT), BF16),
            pltpu.VMEM((TOK, FEAT), BF16),
            pltpu.VMEM((TOK, COLS), F32),
            pltpu.VMEM((TOK, FEAT), BF16),
            pltpu.VMEM((2, TOK, HD), BF16),
            pltpu.VMEM((TOK, COLS), BF16),
            pltpu.VMEM((2, COLS, TOK), BF16),
            pltpu.VMEM((2, TOK, HD), F32),
            pltpu.VMEM((TOK, HD), BF16),
            pltpu.VMEM((TOK, HD), BF16),
            pltpu.VMEM((16, TOK, FEAT), BF16),
            pltpu.VMEM((8, TOK, FEAT), BF16),
            pltpu.VMEM((8, HT, FEAT), BF16),
            pltpu.VMEM((2, TOK, FEAT), BF16),
            pltpu.VMEM((2, HT, FEAT), BF16),
            pltpu.VMEM((8, COLS, FEAT), BF16),
            pltpu.VMEM((4, COLS, FEAT), BF16),
            pltpu.VMEM((4, HG, FEAT), BF16),
            pltpu.VMEM((COLS, FEAT), BF16),
            pltpu.SemaphoreType.DMA((4,)),
            pltpu.SemaphoreType.DMA((N_SEMS,)),
            pltpu.SemaphoreType.DMA((N_SEMS,)),
        ],
        compiler_params=pltpu.CompilerParams(
            collective_id=0, has_side_effects=True, vmem_limit_bytes=60 * 2**20
        ),
        name="attention_backward",
    )(tokens_in, out_grad, q_weight, kv_weight, jnp.asarray(cosine), jnp.asarray(sine))


def solution(mesh):
    spec = P("dp", "tensor")
    return jax.shard_map(
        body, mesh=mesh, in_specs=(spec,) * 4, out_specs=(spec,) * 3, check_vma=False
    )
```

```python
import functools
import jax
import jax.numpy as jnp
import numpy as np
from jax import lax
from jax.sharding import PartitionSpec as P
from jax.experimental import pallas as pl
from jax.experimental.pallas import tpu as pltpu

MESH = pl.DeviceIdType.MESH
F32, BF16 = jnp.float32, jnp.bfloat16
TOK, FEAT, HD, HEADS, COLS = 384, 512, 128, 4, 640
HT, HW, HG = TOK // 2, FEAT // 2, COLS // 2
N_SEMS = 192
LOG2E = float(np.log2(np.e))


def rope_tables(length, size):
    half = size // 2
    positions = np.arange(length, dtype=np.float32)
    inverse = np.power(
        np.float32(500000.0), -(np.arange(half, dtype=np.float32) * np.float32(2.0) / np.float32(size))
    ).astype(np.float32)
    angle = (positions[:, None] * inverse[None, :]).astype(np.float32).astype(np.float64)
    cosine, sine = np.cos(angle), np.sin(angle)
    return (
        np.concatenate([cosine, cosine], axis=1).astype(np.float32),
        np.concatenate([-sine, sine], axis=1).astype(np.float32),
    )


def dot_nn(a, b):
    return lax.dot_general(a, b, (((1,), (0,)), ((), ())), preferred_element_type=F32)


def dot_nt(a, b):
    return lax.dot_general(a, b, (((1,), (1,)), ((), ())), preferred_element_type=F32)


def dot_tn(a, b):
    return lax.dot_general(a, b, (((0,), (0,)), ((), ())), preferred_element_type=F32)


def kernel(
    x_in, og_in, wq_in, wkv_in, cos_in, sin_in,
    dx_out, qg_out, kvg_out,
    cos_ref, sin_ref, dx_st, qg_st, kvg_st,
    xbuf, wbuf, xsib, og, acc, qbuf, kv, gbuf, gt, part, part_low, part_in,
    dxs, ry_full, ry_half, rz_full, rz_half,
    dws, rx_full, rx_half, rzl,
    local_sem, ss, rs,
):
    dp, tn = lax.axis_index("dp"), lax.axis_index("tensor")
    x, zl, c = dp // 4, (dp // 2) % 2, dp % 2
    zh, y = tn // 4, tn % 4
    role = y % 2
    is_key = role == 0

    def wb(dx, dz, dc):
        return ((x + dx) % 4) * 4 + ((zl + dz) % 2) * 2 + (c + dc) % 2

    def tb(dh, dy):
        return ((zh + dh) % 4) * 4 + (y + dy) % 4

    sib = (wb(0, 0, 1), tn)
    zlp = (wb(0, 1, 0), tn)
    xp, xm = (wb(1, 0, 0), tn), (wb(3, 0, 0), tn)
    yp, ym = (dp, tb(0, 1)), (dp, tb(0, 3))
    zp, zm = (dp, tb(1, 0)), (dp, tb(3, 0))
    mate = (dp, zh * 4 + y + 1 - 2 * role)

    names = {}
    pending = []

    def sem(name):
        return names.setdefault(name, len(names))

    def send(name, src, dst, to):
        k = sem(name)
        copy = pltpu.make_async_remote_copy(
            src_ref=src, dst_ref=dst, send_sem=ss.at[k], recv_sem=rs.at[k],
            device_id=to, device_id_type=MESH,
        )
        copy.start()
        pending.append(copy)

    def recv(name, dst):
        k = sem(name)
        pltpu.make_async_remote_copy(
            src_ref=dst, dst_ref=dst, send_sem=ss.at[k], recv_sem=rs.at[k],
            device_id=sib, device_id_type=MESH,
        ).wait_recv()

    def xs(block, h):
        return xbuf.at[block, pl.ds(h * HT, HT)]

    def ws(block, h):
        return wbuf.at[block, pl.ds(h * HW, HW)]

    own_x, own_w = tn, dp
    barrier = pltpu.get_barrier_semaphore()
    neighbours = (sib, zlp, xp, xm, yp, ym, zp, zm)
    for to in neighbours:
        pl.semaphore_signal(barrier, inc=1, device_id=to, device_id_type=MESH)
    loads = [
        pltpu.make_async_copy(x_in, xbuf.at[own_x], local_sem.at[0]),
        pltpu.make_async_copy(wq_in, wbuf.at[own_w, :, pl.ds(0, FEAT)], local_sem.at[1]),
        pltpu.make_async_copy(wkv_in, wbuf.at[own_w, :, pl.ds(FEAT, HD)], local_sem.at[2]),
        pltpu.make_async_copy(og_in, og, local_sem.at[3]),
        pltpu.make_async_copy(cos_in, cos_ref, local_sem.at[4]),
        pltpu.make_async_copy(sin_in, sin_ref, local_sem.at[5]),
    ]
    for load in loads:
        load.start()
    pl.semaphore_wait(barrier, len(neighbours))

    def send_x(name, block, h, to):
        send((name, h), xs(block, h), xs(block, h), to)

    def recv_x(name, block, h):
        recv((name, h), xs(block, h))

    def send_w(name, block, h, to):
        send((name, h), ws(block, h), ws(block, h), to)

    def recv_w(name, block, h):
        recv((name, h), ws(block, h))

    def spread_y(j, h):
        send_x(("yp", j), tb(j, 0), h, yp)
        send_x(("ym", j), tb(j, 0), h, ym)

    loads[0].wait()
    for h in (0, 1):
        send_x("zp", own_x, h, zp)
        send_x("zm", own_x, 1 - h, zm)
        send_x(("yp", 0), own_x, h, yp)
        send_x(("ym", 0), own_x, 1 - h, ym)
    loads[1].wait()
    loads[2].wait()
    for h in (0, 1):
        send_w(("xp", 0), own_w, h, xp)
        send_w(("xm", 0), own_w, 1 - h, xm)
    for h in (0, 1):
        send_w("sib", own_w, h, sib)

    def relay_y(j, which):
        if which == 0:
            recv_x(("yp", j), tb(j, 3), 0)
            send_x(("ypr", j), tb(j, 3), 0, yp)
        else:
            recv_x(("ym", j), tb(j, 1), 1)
            send_x(("ymr", j), tb(j, 1), 1, ym)

    def relay_x(dz, which):
        if which == 0:
            recv_w(("xp", dz), wb(3, dz, 0), 0)
            send_w(("xpr", dz), wb(3, dz, 0), 0, xp)
            send_w(("sxp", dz), wb(3, dz, 0), 0, sib)
        else:
            recv_w(("xm", dz), wb(1, dz, 0), 1)
            send_w(("xmr", dz), wb(1, dz, 0), 1, xm)
            send_w(("sxm", dz), wb(1, dz, 0), 1, sib)

    def rest_x(dz):
        recv_w(("xp", dz), wb(3, dz, 0), 1)
        send_w(("sxp", dz), wb(3, dz, 0), 1, sib)
        recv_w(("xm", dz), wb(1, dz, 0), 0)
        send_w(("sxm", dz), wb(1, dz, 0), 0, sib)

    def far_x(dz):
        recv_w(("xpr", dz), wb(2, dz, 0), 0)
        send_w(("sfar", dz), wb(2, dz, 0), 0, sib)
        recv_w(("xmr", dz), wb(2, dz, 0), 1)
        send_w(("sfar", dz), wb(2, dz, 0), 1, sib)

    def from_zl(h):
        block = wb(0, 1, 0)
        recv_w("zl", block, h)
        send_w(("xp", 1), block, h, xp)
        send_w(("xm", 1), block, h, xm)
        send_w("szl", block, h, sib)

    acc[...] = jnp.zeros_like(acc)
    part[...] = jnp.zeros_like(part)
    for load in loads[3:]:
        load.wait()
    late = ((x + 2) % 4) * 2 + 1 - zl

    def project(b, ready):
        @pl.when(ready)
        def _():
            acc[...] += dot_nn(xbuf[b], wbuf[b])

    def project_row(dh, dz):
        first = ((zh + dh) % 4) * 4

        def one(i, carry):
            b = first + i
            same = (b // 2) % 2 == zl
            project(b, same if dz == 0 else jnp.logical_and(jnp.logical_not(same), b // 2 != late))
            return carry

        lax.fori_loop(0, 4, one, 0)

    def rest_y(j):
        recv_x(("yp", j), tb(j, 3), 1)
        recv_x(("ym", j), tb(j, 1), 0)

    def far_y(j):
        recv_x(("ypr", j), tb(j, 2), 0)
        recv_x(("ymr", j), tb(j, 2), 1)

    relay_y(0, 0)
    relay_y(0, 1)
    relay_x(0, 0)
    relay_x(0, 1)
    recv_x("zp", tb(3, 0), 0)
    spread_y(3, 0)
    recv_x("zm", tb(1, 0), 1)
    spread_y(1, 1)
    send_w("zl", own_w, 0, zlp)
    rest_x(0)
    relay_y(3, 0)
    relay_y(1, 1)
    recv_x("zp", tb(3, 0), 1)
    spread_y(3, 1)
    recv_x("zm", tb(1, 0), 0)
    spread_y(1, 0)
    send_w("zl", own_w, 1, zlp)
    send_x("zpr", tb(3, 0), 0, zp)
    send_x("zmr", tb(1, 0), 1, zm)
    far_x(0)
    from_zl(0)
    relay_y(3, 1)
    relay_y(1, 0)
    from_zl(1)
    rest_y(0)
    far_y(0)
    for h in (0, 1):
        recv_w("sib", wb(0, 0, 1), h)
        recv_w(("sxp", 0), wb(3, 0, 1), h)
        recv_w(("sxm", 0), wb(1, 0, 1), h)
        recv_w(("sfar", 0), wb(2, 0, 1), h)
    recv_x("zpr", tb(2, 0), 0)
    spread_y(2, 0)
    recv_x("zmr", tb(2, 0), 1)
    spread_y(2, 1)
    project_row(0, 0)
    relay_x(1, 0)
    relay_x(1, 1)
    rest_y(3)
    far_y(3)
    project_row(3, 0)
    relay_y(2, 0)
    relay_y(2, 1)
    rest_y(1)
    far_y(1)
    project_row(1, 0)
    rest_x(1)
    for h in (0, 1):
        recv_w("szl", wb(0, 1, 1), h)
        recv_w(("sxp", 1), wb(3, 1, 1), h)
        recv_w(("sxm", 1), wb(1, 1, 1), h)
    project_row(0, 1)
    far_x(1)
    project_row(3, 1)
    project_row(1, 1)
    rest_y(2)
    far_y(2)
    project_row(2, 0)
    project_row(2, 1)
    for h in (0, 1):
        recv_w(("sfar", 1), wb(2, 1, 1), h)
    def last_two(cols):
        b0, b1 = wb(2, 1, 0), wb(2, 1, 1)
        acc[:, cols] += dot_nn(xbuf[b0], wbuf[b0, :, cols]) + dot_nn(xbuf[b1], wbuf[b1, :, cols])

    last_two(slice(FEAT, COLS))

    def rot(u, rows=slice(None)):
        return u * cos_ref[rows, :] + pltpu.roll(u, HD // 2, 1) * sin_ref[rows, :]

    def unrot(u, rows=slice(None)):
        return u * cos_ref[rows, :] - pltpu.roll(u, HD // 2, 1) * sin_ref[rows, :]

    raw = acc[:, FEAT:COLS]
    kv[role] = jnp.where(is_key, rot(raw), raw).astype(BF16)
    send("kv", kv.at[role], kv.at[role], mate)

    for i in range(8):
        send(("xsib", i), xbuf.at[2 * i + 1 - c], xsib.at[i], sib)

    last_two(slice(0, FEAT))
    for h in range(HEADS):
        qbuf[:, h * HD:(h + 1) * HD] = rot(acc[:, h * HD:(h + 1) * HD]).astype(BF16)
    recv("kv", kv.at[1 - role])

    scale = HD ** -0.5

    for i in reversed(range(TOK // HD)):
        rows, n = slice(i * HD, (i + 1) * HD), (i + 1) * HD

        def head(h, carry, i=i, rows=rows, n=n):
            cols = pl.ds(pl.multiple_of(h * HD, HD), HD)
            q, grad = qbuf[rows, cols], og[rows, cols]
            k, v = kv[0, :n], kv[1, :n]
            scores = dot_nt(q, k)
            q_pos = lax.broadcasted_iota(jnp.int32, (HD, n), 0) + i * HD
            k_pos = lax.broadcasted_iota(jnp.int32, (HD, n), 1)
            scores = jnp.where(k_pos <= q_pos, scores, -jnp.inf)
            expo = jnp.exp2((scores - jnp.max(scores, axis=-1, keepdims=True)) * (scale * LOG2E))
            probs = expo * (1.0 / jnp.sum(expo, axis=-1, keepdims=True))
            dprobs = dot_nt(grad, v)
            delta = jnp.sum(probs * dprobs, axis=-1, keepdims=True)
            dscores = (probs * ((dprobs - delta) * scale)).astype(BF16)
            dq = unrot(dot_nn(dscores, k), rows)
            gbuf[rows, cols] = dq.astype(BF16)
            gt[0, cols, rows] = dq.T.astype(BF16)
            part[0, :n] += dot_tn(dscores, q)
            part[1, :n] += dot_tn(probs.astype(BF16), grad)
            return carry

        lax.fori_loop(0, HEADS, head, 0, unroll=2 if i == 2 else 4)
        part_low[rows, :] = part[1 - role, rows, :].astype(BF16)
        send(("part", i), part_low.at[pl.ds(i * HD, HD)], part_in.at[pl.ds(i * HD, HD)], mate)

    send("gt_q", gt.at[0, pl.ds(0, FEAT)], gt.at[1, pl.ds(0, FEAT)], sib)

    first = tb(2, 2)
    first_q = dot_nt(gbuf[:, :FEAT], wbuf[first, :, :FEAT])
    for i in reversed(range(TOK // HD)):
        rows = slice(i * HD, (i + 1) * HD)
        recv(("part", i), part_in.at[pl.ds(i * HD, HD)])
        total = part[role, rows, :] + part_in[rows, :].astype(F32)
        total = jnp.where(is_key, unrot(total, rows), total)
        gbuf[rows, FEAT:COLS] = total.astype(BF16)
        gt[0, FEAT:COLS, rows] = total.T.astype(BF16)
    send("gt_kv", gt.at[0, pl.ds(FEAT, HD)], gt.at[1, pl.ds(FEAT, HD)], sib)

    stores = []

    def store(src, dst):
        copy = pltpu.make_async_copy(src, dst, local_sem.at[len(loads) + len(stores)])
        copy.start()
        stores.append(copy)

    def dx_half(j, dy, h):
        return dot_nt(gbuf[h * HT:(h + 1) * HT, :], wbuf[tb(j, dy)])

    def dw_half(ddx, dz, h):
        b = wb(ddx, dz, 0)
        rows = slice(h * HG, (h + 1) * HG)
        return dot_nn(gt[0, rows, :], xbuf[b]) + dot_nn(gt[1, rows, :], xsib[b // 2])

    def tslot(ref, i, h):
        return ref.at[i, pl.ds(h * HT, HT)]

    def gslot(ref, i, h):
        return ref.at[i, pl.ds(h * HG, HG)]

    def load_t(ref, i, h):
        return ref[i, h * HT:(h + 1) * HT, :].astype(F32)

    def load_g(ref, i, h):
        return ref[i, h * HG:(h + 1) * HG, :].astype(F32)

    def put_dx(name, j, dy, h, value, dst, to):
        i = j * 4 + dy
        dxs[i, h * HT:(h + 1) * HT, :] = value.astype(BF16)
        send(name, tslot(dxs, i, h), dst, to)

    def put_dw(name, ddx, dz, h, value, dst, to):
        i = ddx * 2 + dz
        dws[i, h * HG:(h + 1) * HG, :] = value.astype(BF16)
        send(name, gslot(dws, i, h), dst, to)

    def s1(j0, j1, value0=None, value1=None):
        value0 = dx_half(j0, 2, 0) if value0 is None else value0
        put_dx(("s1", 0, j0), j0, 2, 0, value0, ry_half.at[j0 * 2], yp)
        value1 = dx_half(j1, 2, 1) if value1 is None else value1
        put_dx(("s1", 1, j1), j1, 2, 1, value1, ry_half.at[j1 * 2 + 1], ym)

    def s2n(j0, j1):
        put_dx(("s2", j1, 0, 1), j1, 1, 1, dx_half(j1, 1, 1), tslot(ry_full, j1 * 2, 1), yp)
        put_dx(("s2", j0, 1, 0), j0, 3, 0, dx_half(j0, 3, 0), tslot(ry_full, j0 * 2 + 1, 0), ym)

    def s2d(j0, j1):
        mine = dx_half(j0, 1, 0)
        recv(("s1", 0, j0), ry_half.at[j0 * 2])
        put_dx(("s2", j0, 0, 0), j0, 1, 0, mine + ry_half[j0 * 2].astype(F32), tslot(ry_full, j0 * 2, 0), yp)
        mine = dx_half(j1, 3, 1)
        recv(("s1", 1, j1), ry_half.at[j1 * 2 + 1])
        put_dx(
            ("s2", j1, 1, 1), j1, 3, 1, mine + ry_half[j1 * 2 + 1].astype(F32), tslot(ry_full, j1 * 2 + 1, 1), ym
        )

    def s3(j0, j1):
        for h, j in ((0, j0), (1, j1)):
            mine = dx_half(j, 0, h)
            recv(("s2", j, 0, h), tslot(ry_full, j * 2, h))
            recv(("s2", j, 1, h), tslot(ry_full, j * 2 + 1, h))
            mine = mine + load_t(ry_full, j * 2, h) + load_t(ry_full, j * 2 + 1, h)
            if j == 2:
                put_dx(("z1", h), 2, 0, h, mine, rz_half.at[h], zp if h == 0 else zm)
            elif j == 0:
                recv(("z2", 0, h), tslot(rz_full, 0, h))
                recv(("z2", 1, h), tslot(rz_full, 1, h))
                mine = mine + load_t(rz_full, 0, h) + load_t(rz_full, 1, h)
                dx_st[h * HT:(h + 1) * HT, :] = mine.astype(BF16)
                store(dx_st.at[pl.ds(h * HT, HT)], dx_out.at[pl.ds(h * HT, HT)])
            else:
                side = 0 if j == 1 else 1
                if h == side:
                    recv(("z1", side), rz_half.at[side])
                    mine = mine + rz_half[side].astype(F32)
                put_dx(("z2", side, h), j, 0, h, mine, tslot(rz_full, side, h), zp if j == 1 else zm)

    def t1(dz):
        put_dw(("t1", dz, 0), 2, dz, 0, dw_half(2, dz, 0), rx_half.at[dz * 2], xp)
        put_dw(("t1", dz, 1), 2, dz, 1, dw_half(2, dz, 1), rx_half.at[dz * 2 + 1], xm)

    def t2n(dz):
        put_dw(("t2", dz, 0, 1), 1, dz, 1, dw_half(1, dz, 1), gslot(rx_full, dz * 2, 1), xp)
        put_dw(("t2", dz, 1, 0), 3, dz, 0, dw_half(3, dz, 0), gslot(rx_full, dz * 2 + 1, 0), xm)

    def t2d(dz):
        mine = dw_half(1, dz, 0)
        recv(("t1", dz, 0), rx_half.at[dz * 2])
        put_dw(("t2", dz, 0, 0), 1, dz, 0, mine + rx_half[dz * 2].astype(F32), gslot(rx_full, dz * 2, 0), xp)
        mine = dw_half(3, dz, 1)
        recv(("t1", dz, 1), rx_half.at[dz * 2 + 1])
        put_dw(
            ("t2", dz, 1, 1), 3, dz, 1, mine + rx_half[dz * 2 + 1].astype(F32), gslot(rx_full, dz * 2 + 1, 1), xm
        )

    def t3(dz):
        for h in (0, 1):
            mine = dw_half(0, dz, h)
            recv(("t2", dz, 0, h), gslot(rx_full, dz * 2, h))
            recv(("t2", dz, 1, h), gslot(rx_full, dz * 2 + 1, h))
            mine = mine + load_g(rx_full, dz * 2, h) + load_g(rx_full, dz * 2 + 1, h)
            if dz == 1:
                put_dw(("t3", h), 0, 1, h, mine, rzl.at[pl.ds(h * HG, HG)], zlp)
            else:
                recv(("t3", h), rzl.at[pl.ds(h * HG, HG)])
                mine = (mine + rzl[h * HG:(h + 1) * HG, :].astype(F32)).T.astype(BF16)
                if h == 0:
                    qg_st[:, :HG] = mine
                    store(qg_st.at[:, pl.ds(0, HW)], qg_out.at[:, pl.ds(0, HW)])
                else:
                    qg_st[:, HG:] = mine[:, :FEAT - HG]
                    store(qg_st.at[:, pl.ds(HW, HW)], qg_out.at[:, pl.ds(HW, HW)])
                    kvg_st[...] = mine[:, FEAT - HG:]
                    store(kvg_st, kvg_out)

    first_kv = dot_nt(gbuf[:, FEAT:COLS], wbuf[first, :, FEAT:COLS])
    s1(2, 2, first_q[:HT] + first_kv[:HT], first_q[HT:] + first_kv[HT:])
    for i in range(8):
        recv(("xsib", i), xsib.at[i])
    recv("gt_q", gt.at[1, pl.ds(0, FEAT)])
    recv("gt_kv", gt.at[1, pl.ds(FEAT, HD)])
    t1(1)
    s2n(2, 2)
    t2n(1)
    s1(3, 1)
    s2d(2, 2)
    s2n(3, 1)
    t2d(1)
    t1(0)
    s1(1, 3)
    s2d(3, 1)
    s3(2, 2)
    s2n(1, 3)
    t2n(0)
    t3(1)
    s1(0, 0)
    s2d(1, 3)
    t2d(0)
    s3(3, 1)
    s2n(0, 0)
    s2d(0, 0)
    s3(1, 3)
    t3(0)
    s3(0, 0)

    for copy in stores:
        copy.wait()
    for copy in pending:
        copy.wait_send()
    assert len(names) <= N_SEMS


def hand_on(*refs):
    n = len(refs) // 3
    sources, targets, held = refs[:n], refs[n:2 * n], refs[2 * n:3 * n]
    sem_in, sem_out = refs[3 * n:]
    steps = []
    for i in range(n):
        size = held[i].shape[0] // 2
        for h in (0, 1):
            k, rows = 2 * i + h, pl.ds(h * size, size)
            steps.append((
                pltpu.make_async_copy(sources[i].at[rows], held[i].at[rows], sem_in.at[k]),
                pltpu.make_async_copy(held[i].at[rows], targets[i].at[rows], sem_out.at[k]),
            ))
    for into, _ in steps:
        into.start()
    for into, out in steps:
        into.wait()
        out.start()
    for _, out in steps:
        out.wait()


def body(tokens_in, out_grad, q_weight, kv_weight):
    cosine, sine = rope_tables(TOK, HD)
    anywhere = pl.BlockSpec(memory_space=pl.ANY)
    outs = (
        jax.ShapeDtypeStruct((TOK, FEAT), BF16),
        jax.ShapeDtypeStruct((FEAT, FEAT), BF16),
        jax.ShapeDtypeStruct((FEAT, HD), BF16),
    )
    results = pl.pallas_call(
        kernel,
        out_shape=outs,
        in_specs=[anywhere] * 6,
        out_specs=(anywhere,) * 3,
        scratch_shapes=[
            pltpu.VMEM((TOK, HD), F32),
            pltpu.VMEM((TOK, HD), F32),
            pltpu.VMEM((TOK, FEAT), BF16),
            pltpu.VMEM((FEAT, FEAT), BF16),
            pltpu.VMEM((FEAT, HD), BF16),
            pltpu.VMEM((16, TOK, FEAT), BF16),
            pltpu.VMEM((16, FEAT, COLS), BF16),
            pltpu.VMEM((8, TOK, FEAT), BF16),
            pltpu.VMEM((TOK, FEAT), BF16),
            pltpu.VMEM((TOK, COLS), F32),
            pltpu.VMEM((TOK, FEAT), BF16),
            pltpu.VMEM((2, TOK, HD), BF16),
            pltpu.VMEM((TOK, COLS), BF16),
            pltpu.VMEM((2, COLS, TOK), BF16),
            pltpu.VMEM((2, TOK, HD), F32),
            pltpu.VMEM((TOK, HD), BF16),
            pltpu.VMEM((TOK, HD), BF16),
            pltpu.VMEM((16, TOK, FEAT), BF16),
            pltpu.VMEM((8, TOK, FEAT), BF16),
            pltpu.VMEM((8, HT, FEAT), BF16),
            pltpu.VMEM((2, TOK, FEAT), BF16),
            pltpu.VMEM((2, HT, FEAT), BF16),
            pltpu.VMEM((8, COLS, FEAT), BF16),
            pltpu.VMEM((4, COLS, FEAT), BF16),
            pltpu.VMEM((4, HG, FEAT), BF16),
            pltpu.VMEM((COLS, FEAT), BF16),
            pltpu.SemaphoreType.DMA((12,)),
            pltpu.SemaphoreType.DMA((N_SEMS,)),
            pltpu.SemaphoreType.DMA((N_SEMS,)),
        ],
        compiler_params=pltpu.CompilerParams(
            collective_id=0, has_side_effects=True, vmem_limit_bytes=60 * 2**20
        ),
        name="attention_backward",
    )(tokens_in, out_grad, q_weight, kv_weight, jnp.asarray(cosine), jnp.asarray(sine))
    return pl.pallas_call(
        hand_on,
        out_shape=outs,
        in_specs=[anywhere] * 3,
        out_specs=(anywhere,) * 3,
        scratch_shapes=[pltpu.VMEM(o.shape, o.dtype) for o in outs] + [pltpu.SemaphoreType.DMA((6,))] * 2,
        name="hand_on",
    )(*results)


def solution(mesh):
    spec = P("dp", "tensor")
    return jax.shard_map(
        body, mesh=mesh, in_specs=(spec,) * 4, out_specs=(spec,) * 3, check_vma=False
    )
```

```python
import functools
import jax
import jax.numpy as jnp
import numpy as np
from jax import lax
from jax.sharding import PartitionSpec as P
from jax.experimental import pallas as pl
from jax.experimental.pallas import tpu as pltpu

MESH = pl.DeviceIdType.MESH
F32, BF16 = jnp.float32, jnp.bfloat16
TOK, FEAT, HD, HEADS, COLS = 384, 512, 128, 4, 640
HT, HW = TOK // 2, FEAT // 2
GC, GH = COLS // 2, COLS // 4
CHUNKS = ((0, HD), (2 * HD, HD // 2))
N_SEMS = 162
N_SEND = 56
LOG2E = float(np.log2(np.e))


def rope_tables(length, size):
    half = size // 2
    positions = np.arange(length, dtype=np.float32)
    inverse = np.power(
        np.float32(500000.0), -(np.arange(half, dtype=np.float32) * np.float32(2.0) / np.float32(size))
    ).astype(np.float32)
    angle = (positions[:, None] * inverse[None, :]).astype(np.float32).astype(np.float64)
    cosine, sine = np.cos(angle), np.sin(angle)
    return (
        np.concatenate([cosine, cosine], axis=1).astype(np.float32),
        np.concatenate([-sine, sine], axis=1).astype(np.float32),
    )


def dot_nn(a, b):
    return lax.dot_general(a, b, (((1,), (0,)), ((), ())), preferred_element_type=F32)


def dot_nt(a, b):
    return lax.dot_general(a, b, (((1,), (1,)), ((), ())), preferred_element_type=F32)


def dot_tn(a, b):
    return lax.dot_general(a, b, (((0,), (0,)), ((), ())), preferred_element_type=F32)


def kernel(
    x_in, og_in, wq_in, wkv_in, cos_in, sin_in,
    dx_out, qg_out, kvg_out,
    cos_ref, sin_ref, dx_st, qg_st, kvg_st, t_st,
    xbuf, wbuf, xsib, og, acc, qbuf, kv, gbuf, gt, part, part_low, part_in,
    dxs, ry_full, ry_half, rz_full, rz_half,
    dws, rx_full, rx_half, rzl,
    local_sem, ss, rs,
):
    dp, tn = lax.axis_index("dp"), lax.axis_index("tensor")
    x, zl, c = dp // 4, (dp // 2) % 2, dp % 2
    zh, y = tn // 4, tn % 4
    role = y % 2
    is_key = role == 0

    def wb(dx, dz, dc):
        return ((x + dx) % 4) * 4 + ((zl + dz) % 2) * 2 + (c + dc) % 2

    def tb(dh, dy):
        return ((zh + dh) % 4) * 4 + (y + dy) % 4

    sib = (wb(0, 0, 1), tn)
    zlp = (wb(0, 1, 0), tn)
    xp, xm = (wb(1, 0, 0), tn), (wb(3, 0, 0), tn)
    yp, ym = (dp, tb(0, 1)), (dp, tb(0, 3))
    zp, zm = (dp, tb(1, 0)), (dp, tb(3, 0))
    mate = (dp, zh * 4 + y + 1 - 2 * role)

    names = {}
    pending = []

    def sem(name):
        return names.setdefault(name, len(names))

    def send(name, src, dst, to):
        k, n = sem(name), len(pending)
        if n >= N_SEND:
            pending[n - N_SEND].wait_send()
        copy = pltpu.make_async_remote_copy(
            src_ref=src, dst_ref=dst, send_sem=ss.at[n % N_SEND], recv_sem=rs.at[k],
            device_id=to, device_id_type=MESH,
        )
        copy.start()
        pending.append(copy)

    def recv(name, dst):
        k = sem(name)
        pltpu.make_async_remote_copy(
            src_ref=dst, dst_ref=dst, send_sem=ss.at[0], recv_sem=rs.at[k],
            device_id=sib, device_id_type=MESH,
        ).wait_recv()

    def xs(block, h):
        return xbuf.at[block, pl.ds(h * HT, HT)]

    def ws(block, h):
        return wbuf.at[block, pl.ds(h * HW, HW)]

    own_x, own_w = tn, dp
    barrier = pltpu.get_barrier_semaphore()
    neighbours = (sib, zlp, xp, xm, yp, ym, zp, zm)
    for to in neighbours:
        pl.semaphore_signal(barrier, inc=1, device_id=to, device_id_type=MESH)
    loads = [
        pltpu.make_async_copy(x_in, xbuf.at[own_x], local_sem.at[0]),
        pltpu.make_async_copy(wq_in, wbuf.at[own_w, :, pl.ds(0, FEAT)], local_sem.at[1]),
        pltpu.make_async_copy(wkv_in, wbuf.at[own_w, :, pl.ds(FEAT, HD)], local_sem.at[2]),
        pltpu.make_async_copy(og_in, og, local_sem.at[3]),
        pltpu.make_async_copy(cos_in, cos_ref, local_sem.at[4]),
        pltpu.make_async_copy(sin_in, sin_ref, local_sem.at[5]),
    ]
    for load in loads:
        load.start()
    pl.semaphore_wait(barrier, len(neighbours))

    def send_x(name, block, h, to):
        send((name, h), xs(block, h), xs(block, h), to)

    def recv_x(name, block, h):
        recv((name, h), xs(block, h))

    def send_w(name, block, h, to):
        send((name, h), ws(block, h), ws(block, h), to)

    def recv_w(name, block, h):
        recv((name, h), ws(block, h))

    def spread_y(j, h):
        send_x(("yp", j), tb(j, 0), h, yp)
        send_x(("ym", j), tb(j, 0), h, ym)

    loads[0].wait()
    for h in (0, 1):
        send_x("zp", own_x, h, zp)
        send_x("zm", own_x, 1 - h, zm)
        send_x(("yp", 0), own_x, h, yp)
        send_x(("ym", 0), own_x, 1 - h, ym)
    loads[1].wait()
    loads[2].wait()
    for h in (0, 1):
        send_w(("xp", 0), own_w, h, xp)
        send_w(("xm", 0), own_w, 1 - h, xm)
    for h in (0, 1):
        send_w("sib", own_w, h, sib)

    def relay_y(j, which):
        if which == 0:
            recv_x(("yp", j), tb(j, 3), 0)
            send_x(("ypr", j), tb(j, 3), 0, yp)
        else:
            recv_x(("ym", j), tb(j, 1), 1)
            send_x(("ymr", j), tb(j, 1), 1, ym)

    def relay_x(dz, which):
        if which == 0:
            recv_w(("xp", dz), wb(3, dz, 0), 0)
            send_w(("xpr", dz), wb(3, dz, 0), 0, xp)
            send_w(("sxp", dz), wb(3, dz, 0), 0, sib)
        else:
            recv_w(("xm", dz), wb(1, dz, 0), 1)
            send_w(("xmr", dz), wb(1, dz, 0), 1, xm)
            send_w(("sxm", dz), wb(1, dz, 0), 1, sib)

    def rest_x(dz):
        recv_w(("xp", dz), wb(3, dz, 0), 1)
        send_w(("sxp", dz), wb(3, dz, 0), 1, sib)
        recv_w(("xm", dz), wb(1, dz, 0), 0)
        send_w(("sxm", dz), wb(1, dz, 0), 0, sib)

    def far_x(dz):
        recv_w(("xpr", dz), wb(2, dz, 0), 0)
        send_w(("sfar", dz), wb(2, dz, 0), 0, sib)
        recv_w(("xmr", dz), wb(2, dz, 0), 1)
        send_w(("sfar", dz), wb(2, dz, 0), 1, sib)

    def from_zl(h):
        block = wb(0, 1, 0)
        recv_w("zl", block, h)
        send_w(("xp", 1), block, h, xp)
        send_w(("xm", 1), block, h, xm)
        send_w("szl", block, h, sib)

    acc[...] = jnp.zeros_like(acc)
    part[...] = jnp.zeros_like(part)
    for load in loads[3:]:
        load.wait()
    late = ((x + 2) % 4) * 2 + 1 - zl

    def project(b, ready):
        @pl.when(ready)
        def _():
            acc[...] += dot_nn(xbuf[b], wbuf[b])

    def project_row(dh, dz):
        first = ((zh + dh) % 4) * 4

        def one(i, carry):
            b = first + i
            same = (b // 2) % 2 == zl
            project(b, same if dz == 0 else jnp.logical_and(jnp.logical_not(same), b // 2 != late))
            return carry

        lax.fori_loop(0, 4, one, 0)

    def rest_y(j):
        recv_x(("yp", j), tb(j, 3), 1)
        recv_x(("ym", j), tb(j, 1), 0)

    def far_y(j):
        recv_x(("ypr", j), tb(j, 2), 0)
        recv_x(("ymr", j), tb(j, 2), 1)

    relay_y(0, 0)
    relay_y(0, 1)
    relay_x(0, 0)
    relay_x(0, 1)
    recv_x("zp", tb(3, 0), 0)
    spread_y(3, 0)
    recv_x("zm", tb(1, 0), 1)
    spread_y(1, 1)
    send_w("zl", own_w, 0, zlp)
    rest_x(0)
    relay_y(3, 0)
    relay_y(1, 1)
    recv_x("zp", tb(3, 0), 1)
    spread_y(3, 1)
    recv_x("zm", tb(1, 0), 0)
    spread_y(1, 0)
    send_w("zl", own_w, 1, zlp)
    send_x("zpr", tb(3, 0), 0, zp)
    send_x("zmr", tb(1, 0), 1, zm)
    far_x(0)
    from_zl(0)
    relay_y(3, 1)
    relay_y(1, 0)
    from_zl(1)
    rest_y(0)
    far_y(0)
    for h in (0, 1):
        recv_w("sib", wb(0, 0, 1), h)
        recv_w(("sxp", 0), wb(3, 0, 1), h)
        recv_w(("sxm", 0), wb(1, 0, 1), h)
        recv_w(("sfar", 0), wb(2, 0, 1), h)
    recv_x("zpr", tb(2, 0), 0)
    spread_y(2, 0)
    recv_x("zmr", tb(2, 0), 1)
    spread_y(2, 1)
    project_row(0, 0)
    relay_x(1, 0)
    relay_x(1, 1)
    rest_y(3)
    far_y(3)
    project_row(3, 0)
    relay_y(2, 0)
    relay_y(2, 1)
    rest_y(1)
    far_y(1)
    project_row(1, 0)
    rest_x(1)
    for h in (0, 1):
        recv_w("szl", wb(0, 1, 1), h)
        recv_w(("sxp", 1), wb(3, 1, 1), h)
        recv_w(("sxm", 1), wb(1, 1, 1), h)
    project_row(0, 1)
    far_x(1)
    project_row(3, 1)
    project_row(1, 1)
    rest_y(2)
    far_y(2)
    project_row(2, 0)
    project_row(2, 1)
    for h in (0, 1):
        recv_w(("sfar", 1), wb(2, 1, 1), h)
    def last_two(cols):
        b0, b1 = wb(2, 1, 0), wb(2, 1, 1)
        acc[:, cols] += dot_nn(xbuf[b0], wbuf[b0, :, cols]) + dot_nn(xbuf[b1], wbuf[b1, :, cols])

    last_two(slice(FEAT, COLS))

    def rot(u, rows=slice(None)):
        return u * cos_ref[rows, :] + pltpu.roll(u, HD // 2, 1) * sin_ref[rows, :]

    def unrot(u, rows=slice(None)):
        return u * cos_ref[rows, :] - pltpu.roll(u, HD // 2, 1) * sin_ref[rows, :]

    raw = acc[:, FEAT:COLS]
    kv[role] = jnp.where(is_key, rot(raw), raw).astype(BF16)
    send("kv", kv.at[role], kv.at[role], mate)

    for i in range(8):
        send(("xsib", i), xbuf.at[2 * i + 1 - c], xsib.at[i], sib)

    last_two(slice(0, FEAT))
    for h in range(HEADS):
        qbuf[:, h * HD:(h + 1) * HD] = rot(acc[:, h * HD:(h + 1) * HD]).astype(BF16)
    recv("kv", kv.at[1 - role])

    stores = []

    def store(src, dst):
        copy = pltpu.make_async_copy(src, dst, local_sem.at[len(loads) + len(stores)])
        copy.start()
        stores.append(copy)

    def t_rows(ch, h):
        first, size = CHUNKS[ch]
        return slice(first + h * size, first + (h + 1) * size)

    def t_part(ch):
        return slice(0, HD) if ch == 0 else slice(HD, HD + HD // 2)

    def g_rows(ch, h):
        return slice(ch * GC + h * GH, ch * GC + (h + 1) * GH)

    def g_part(ch):
        return slice(ch * GH, (ch + 1) * GH)

    def at(ref, i, rows):
        return ref.at[i, pl.ds(rows.start, rows.stop - rows.start)]

    def value(ref, i, rows):
        return ref[i, rows, :].astype(F32)

    def dx_half(j, dy, ch, h):
        return dot_nt(gbuf[t_rows(ch, h), :], wbuf[tb(j, dy)])

    def dw_half(ddx, dz, ch, h):
        b, rows = wb(ddx, dz, 0), g_rows(ch, h)
        return dot_nn(gt[0, rows, :], xbuf[b]) + dot_nn(gt[1, rows, :], xsib[b // 2])

    def put_dx(name, j, dy, ch, h, mine, dst, to):
        i, rows = j * 4 + dy, t_rows(ch, h)
        dxs[i, rows, :] = mine.astype(BF16)
        send(name, at(dxs, i, rows), dst, to)

    def put_dw(name, ddx, dz, ch, h, mine, dst, to):
        i, rows = ddx * 2 + dz, g_rows(ch, h)
        dws[i, rows, :] = mine.astype(BF16)
        send(name, at(dws, i, rows), dst, to)

    def s1(ch, j0, j1):
        for h, j, to in ((0, j0, yp), (1, j1, ym)):
            put_dx(("s1", h, j, ch), j, 2, ch, h, dx_half(j, 2, ch, h), at(ry_half, j * 2 + h, t_part(ch)), to)

    def s2n(ch, j0, j1):
        for h, j, dy, way, to in ((1, j1, 1, 0, yp), (0, j0, 3, 1, ym)):
            dst = at(ry_full, j * 2 + way, t_rows(ch, h))
            put_dx(("s2", j, way, h, ch), j, dy, ch, h, dx_half(j, dy, ch, h), dst, to)

    def s2d(ch, j0, j1):
        for h, j, dy, to in ((0, j0, 1, yp), (1, j1, 3, ym)):
            mine = dx_half(j, dy, ch, h)
            recv(("s1", h, j, ch), at(ry_half, j * 2 + h, t_part(ch)))
            mine = mine + value(ry_half, j * 2 + h, t_part(ch))
            put_dx(("s2", j, h, h, ch), j, dy, ch, h, mine, at(ry_full, j * 2 + h, t_rows(ch, h)), to)

    def s3(ch, j0, j1):
        for h, j in ((0, j0), (1, j1)):
            rows = t_rows(ch, h)
            mine = dx_half(j, 0, ch, h)
            for way in (0, 1):
                recv(("s2", j, way, h, ch), at(ry_full, j * 2 + way, rows))
                mine = mine + value(ry_full, j * 2 + way, rows)
            if j == 2:
                put_dx(("z1", h, ch), j, 0, ch, h, mine, at(rz_half, h, t_part(ch)), zp if h == 0 else zm)
            elif j == 0:
                for way in (0, 1):
                    recv(("z2", way, h, ch), at(rz_full, way, rows))
                    mine = mine + value(rz_full, way, rows)
                dx_st[rows, :] = mine.astype(BF16)
                part_rows = pl.ds(rows.start, rows.stop - rows.start)
                store(dx_st.at[part_rows], dx_out.at[part_rows])
            else:
                way = 0 if j == 1 else 1
                if h == way:
                    recv(("z1", h, ch), at(rz_half, h, t_part(ch)))
                    mine = mine + value(rz_half, h, t_part(ch))
                put_dx(("z2", way, h, ch), j, 0, ch, h, mine, at(rz_full, way, rows), zp if j == 1 else zm)

    def t1(dz, ch):
        for h, to in ((0, xp), (1, xm)):
            put_dw(("t1", h, dz, ch), 2, dz, ch, h, dw_half(2, dz, ch, h), at(rx_half, dz * 2 + h, g_part(ch)), to)

    def t2n(dz, ch):
        for h, ddx, way, to in ((1, 1, 0, xp), (0, 3, 1, xm)):
            dst = at(rx_full, dz * 2 + way, g_rows(ch, h))
            put_dw(("t2", dz, way, h, ch), ddx, dz, ch, h, dw_half(ddx, dz, ch, h), dst, to)

    def t2d(dz, ch):
        for h, ddx, to in ((0, 1, xp), (1, 3, xm)):
            mine = dw_half(ddx, dz, ch, h)
            recv(("t1", h, dz, ch), at(rx_half, dz * 2 + h, g_part(ch)))
            mine = mine + value(rx_half, dz * 2 + h, g_part(ch))
            put_dw(("t2", dz, h, h, ch), ddx, dz, ch, h, mine, at(rx_full, dz * 2 + h, g_rows(ch, h)), to)

    def t3(dz, ch):
        for h in (0, 1):
            rows = g_rows(ch, h)
            mine = dw_half(0, dz, ch, h)
            for way in (0, 1):
                recv(("t2", dz, way, h, ch), at(rx_full, dz * 2 + way, rows))
                mine = mine + value(rx_full, dz * 2 + way, rows)
            if dz == 1:
                put_dw(("t3", h, ch), 0, 1, ch, h, mine, at(rzl, 0, rows), zlp)
            else:
                recv(("t3", h, ch), at(rzl, 0, rows))
                t_st[rows, :] = mine + value(rzl, 0, rows)
                for k in range(rows.start // HD, rows.stop // HD):
                    block = t_st[k * HD:(k + 1) * HD, :].T.astype(BF16)
                    if k < HEADS:
                        qg_st[:, k * HD:(k + 1) * HD] = block
                        store(qg_st.at[:, pl.ds(k * HD, HD)], qg_out.at[:, pl.ds(k * HD, HD)])
                    else:
                        kvg_st[...] = block
                        store(kvg_st, kvg_out)

    scale = HD ** -0.5

    def finish_role(i):
        rows = slice(i * HD, (i + 1) * HD)
        recv(("part", i), part_in.at[pl.ds(i * HD, HD)])
        total = part[role, rows, :] + part_in[rows, :].astype(F32)
        total = jnp.where(is_key, unrot(total, rows), total)
        gbuf[rows, FEAT:COLS] = total.astype(BF16)
        gt[0, FEAT:COLS, rows] = total.T.astype(BF16)

    for i in reversed(range(TOK // HD)):
        rows, n = slice(i * HD, (i + 1) * HD), (i + 1) * HD

        def head(h, carry, i=i, rows=rows, n=n):
            cols = pl.ds(pl.multiple_of(h * HD, HD), HD)
            q, grad = qbuf[rows, cols], og[rows, cols]
            k, v = kv[0, :n], kv[1, :n]
            scores = dot_nt(q, k)
            q_pos = lax.broadcasted_iota(jnp.int32, (HD, n), 0) + i * HD
            k_pos = lax.broadcasted_iota(jnp.int32, (HD, n), 1)
            scores = jnp.where(k_pos <= q_pos, scores, -jnp.inf)
            expo = jnp.exp2((scores - jnp.max(scores, axis=-1, keepdims=True)) * (scale * LOG2E))
            probs = expo * (1.0 / jnp.sum(expo, axis=-1, keepdims=True))
            dprobs = dot_nt(grad, v)
            delta = jnp.sum(probs * dprobs, axis=-1, keepdims=True)
            dscores = (probs * ((dprobs - delta) * scale)).astype(BF16)
            dq = unrot(dot_nn(dscores, k), rows)
            gbuf[rows, cols] = dq.astype(BF16)
            gt[0, cols, rows] = dq.T.astype(BF16)
            part[0, :n] += dot_tn(dscores, q)
            part[1, :n] += dot_tn(probs.astype(BF16), grad)
            return carry

        lax.fori_loop(0, HEADS, head, 0, unroll=2 if i == 2 else 4)
        part_low[rows, :] = part[1 - role, rows, :].astype(BF16)
        send(("part", i), part_low.at[pl.ds(i * HD, HD)], part_in.at[pl.ds(i * HD, HD)], mate)
        if i == 1:
            finish_role(2)
            s1(1, 2, 2)
            s2n(1, 2, 2)
            s1(1, 3, 1)

    send("gt_q", gt.at[0, pl.ds(0, FEAT)], gt.at[1, pl.ds(0, FEAT)], sib)
    s2d(1, 2, 2)
    for i in range(8):
        recv(("xsib", i), xsib.at[i])
    recv("gt_q", gt.at[1, pl.ds(0, FEAT)])
    t1(1, 0)
    t2n(1, 0)
    finish_role(1)
    finish_role(0)
    send("gt_kv", gt.at[0, pl.ds(FEAT, HD)], gt.at[1, pl.ds(FEAT, HD)], sib)
    s1(0, 2, 2)
    s2n(1, 3, 1)
    s3(1, 2, 2)
    t2d(1, 0)
    s2n(0, 2, 2)
    recv("gt_kv", gt.at[1, pl.ds(FEAT, HD)])
    t1(1, 1)
    s2d(1, 3, 1)
    s1(1, 1, 3)
    t2n(1, 1)
    s2n(1, 1, 3)
    s2d(0, 2, 2)
    s1(0, 3, 1)
    s3(1, 3, 1)
    t3(1, 0)
    t2d(1, 1)
    t1(0, 0)
    s2d(1, 1, 3)
    s2n(0, 3, 1)
    s3(0, 2, 2)
    s2d(0, 3, 1)
    t2n(0, 0)
    s1(0, 1, 3)
    s2n(0, 1, 3)
    t2d(0, 0)
    t1(0, 1)
    s3(1, 1, 3)
    s3(0, 3, 1)
    t3(1, 1)
    s2d(0, 1, 3)
    t2n(0, 1)
    s1(1, 0, 0)
    s2n(1, 0, 0)
    s1(0, 0, 0)
    s2n(0, 0, 0)
    t2d(0, 1)
    s2d(1, 0, 0)
    t3(0, 0)
    s3(0, 1, 3)
    s2d(0, 0, 0)
    s3(1, 0, 0)
    t3(0, 1)
    s3(0, 0, 0)

    for copy in stores:
        copy.wait()
    for copy in pending[-N_SEND:]:
        copy.wait_send()
    assert len(names) <= N_SEMS


def hand_on(*refs):
    n = len(refs) // 3
    sources, targets, held = refs[:n], refs[n:2 * n], refs[2 * n:3 * n]
    sem_in, sem_out = refs[3 * n:]
    steps = []
    for i in range(n):
        size = held[i].shape[0] // 2
        for h in (0, 1):
            k, rows = 2 * i + h, pl.ds(h * size, size)
            steps.append((
                pltpu.make_async_copy(sources[i].at[rows], held[i].at[rows], sem_in.at[k]),
                pltpu.make_async_copy(held[i].at[rows], targets[i].at[rows], sem_out.at[k]),
            ))
    for into, _ in steps:
        into.start()
    for into, out in steps:
        into.wait()
        out.start()
    for _, out in steps:
        out.wait()


def body(tokens_in, out_grad, q_weight, kv_weight):
    cosine, sine = rope_tables(TOK, HD)
    anywhere = pl.BlockSpec(memory_space=pl.ANY)
    outs = (
        jax.ShapeDtypeStruct((TOK, FEAT), BF16),
        jax.ShapeDtypeStruct((FEAT, FEAT), BF16),
        jax.ShapeDtypeStruct((FEAT, HD), BF16),
    )
    results = pl.pallas_call(
        kernel,
        out_shape=outs,
        in_specs=[anywhere] * 6,
        out_specs=(anywhere,) * 3,
        scratch_shapes=[
            pltpu.VMEM((TOK, HD), F32),
            pltpu.VMEM((TOK, HD), F32),
            pltpu.VMEM((TOK, FEAT), BF16),
            pltpu.VMEM((FEAT, FEAT), BF16),
            pltpu.VMEM((FEAT, HD), BF16),
            pltpu.VMEM((COLS, FEAT), F32),
            pltpu.VMEM((16, TOK, FEAT), BF16),
            pltpu.VMEM((16, FEAT, COLS), BF16),
            pltpu.VMEM((8, TOK, FEAT), BF16),
            pltpu.VMEM((TOK, FEAT), BF16),
            pltpu.VMEM((TOK, COLS), F32),
            pltpu.VMEM((TOK, FEAT), BF16),
            pltpu.VMEM((2, TOK, HD), BF16),
            pltpu.VMEM((TOK, COLS), BF16),
            pltpu.VMEM((2, COLS, TOK), BF16),
            pltpu.VMEM((2, TOK, HD), F32),
            pltpu.VMEM((TOK, HD), BF16),
            pltpu.VMEM((TOK, HD), BF16),
            pltpu.VMEM((16, TOK, FEAT), BF16),
            pltpu.VMEM((8, TOK, FEAT), BF16),
            pltpu.VMEM((8, HT, FEAT), BF16),
            pltpu.VMEM((2, TOK, FEAT), BF16),
            pltpu.VMEM((2, HT, FEAT), BF16),
            pltpu.VMEM((8, COLS, FEAT), BF16),
            pltpu.VMEM((4, COLS, FEAT), BF16),
            pltpu.VMEM((4, GC, FEAT), BF16),
            pltpu.VMEM((1, COLS, FEAT), BF16),
            pltpu.SemaphoreType.DMA((16,)),
            pltpu.SemaphoreType.DMA((N_SEND,)),
            pltpu.SemaphoreType.DMA((N_SEMS,)),
        ],
        compiler_params=pltpu.CompilerParams(
            collective_id=0, has_side_effects=True, vmem_limit_bytes=60 * 2**20
        ),
        name="attention_backward",
    )(tokens_in, out_grad, q_weight, kv_weight, jnp.asarray(cosine), jnp.asarray(sine))
    return pl.pallas_call(
        hand_on,
        out_shape=outs,
        in_specs=[anywhere] * 3,
        out_specs=(anywhere,) * 3,
        scratch_shapes=[pltpu.VMEM(o.shape, o.dtype) for o in outs] + [pltpu.SemaphoreType.DMA((6,))] * 2,
        name="hand_on",
    )(*results)


def solution(mesh):
    spec = P("dp", "tensor")
    return jax.shard_map(
        body, mesh=mesh, in_specs=(spec,) * 4, out_specs=(spec,) * 3, check_vma=False
    )
```

```python
import functools
import jax
import jax.numpy as jnp
import numpy as np
from jax import lax
from jax.sharding import PartitionSpec as P
from jax.experimental import pallas as pl
from jax.experimental.pallas import tpu as pltpu

MESH = pl.DeviceIdType.MESH
F32, BF16 = jnp.float32, jnp.bfloat16
TOK, FEAT, HD, HEADS, COLS = 384, 512, 128, 4, 640
HT, HW = TOK // 2, FEAT // 2
GC, GH = COLS // 2, COLS // 4
CHUNKS = ((0, HD), (2 * HD, HD // 2))
LAST = 32
MOST = TOK - LAST
N_SEMS = 166
N_SEND = 56
LOG2E = float(np.log2(np.e))


def rope_tables(length, size):
    half = size // 2
    positions = np.arange(length, dtype=np.float32)
    inverse = np.power(
        np.float32(500000.0), -(np.arange(half, dtype=np.float32) * np.float32(2.0) / np.float32(size))
    ).astype(np.float32)
    angle = (positions[:, None] * inverse[None, :]).astype(np.float32).astype(np.float64)
    cosine, sine = np.cos(angle), np.sin(angle)
    return (
        np.concatenate([cosine, cosine], axis=1).astype(np.float32),
        np.concatenate([-sine, sine], axis=1).astype(np.float32),
    )


def dot_nn(a, b):
    return lax.dot_general(a, b, (((1,), (0,)), ((), ())), preferred_element_type=F32)


def dot_nt(a, b):
    return lax.dot_general(a, b, (((1,), (1,)), ((), ())), preferred_element_type=F32)


def dot_tn(a, b):
    return lax.dot_general(a, b, (((0,), (0,)), ((), ())), preferred_element_type=F32)


def kernel(
    x_in, og_in, wq_in, wkv_in, cos_in, sin_in,
    dx_out, qg_out, kvg_out,
    cos_ref, sin_ref, dx_st, qg_st, kvg_st, t_st,
    xbuf, wbuf, xsib, og, acc, qbuf, kv, gbuf, gt, part, part_low, part_in,
    dxs, ry_full, ry_half, rz_full, rz_half, rq_full, rq_half,
    dws, rx_full, rx_half, rzl,
    local_sem, ss, rs,
):
    dp, tn = lax.axis_index("dp"), lax.axis_index("tensor")
    x, zl, c = dp // 4, (dp // 2) % 2, dp % 2
    zh, y = tn // 4, tn % 4
    role = y % 2
    is_key = role == 0

    def wb(dx, dz, dc):
        return ((x + dx) % 4) * 4 + ((zl + dz) % 2) * 2 + (c + dc) % 2

    def tb(dh, dy):
        return ((zh + dh) % 4) * 4 + (y + dy) % 4

    sib = (wb(0, 0, 1), tn)
    zlp = (wb(0, 1, 0), tn)
    xp, xm = (wb(1, 0, 0), tn), (wb(3, 0, 0), tn)
    yp, ym = (dp, tb(0, 1)), (dp, tb(0, 3))
    zp, zm = (dp, tb(1, 0)), (dp, tb(3, 0))
    mate = (dp, zh * 4 + y + 1 - 2 * role)

    names = {}
    pending = []

    def sem(name):
        return names.setdefault(name, len(names))

    def send(name, src, dst, to):
        k, n = sem(name), len(pending)
        if n >= N_SEND:
            pending[n - N_SEND].wait_send()
        copy = pltpu.make_async_remote_copy(
            src_ref=src, dst_ref=dst, send_sem=ss.at[n % N_SEND], recv_sem=rs.at[k],
            device_id=to, device_id_type=MESH,
        )
        copy.start()
        pending.append(copy)

    def recv(name, dst):
        k = sem(name)
        pltpu.make_async_remote_copy(
            src_ref=dst, dst_ref=dst, send_sem=ss.at[0], recv_sem=rs.at[k],
            device_id=sib, device_id_type=MESH,
        ).wait_recv()

    def xs(block, h):
        return xbuf.at[block, pl.ds(h * HT, HT)]

    def ws(block, h):
        return wbuf.at[block, pl.ds(h * HW, HW)]

    own_x, own_w = tn, dp
    barrier = pltpu.get_barrier_semaphore()
    neighbours = (sib, zlp, xp, xm, yp, ym, zp, zm)
    for to in neighbours:
        pl.semaphore_signal(barrier, inc=1, device_id=to, device_id_type=MESH)
    loads = [
        pltpu.make_async_copy(x_in, xbuf.at[own_x], local_sem.at[0]),
        pltpu.make_async_copy(wq_in, wbuf.at[own_w, :, pl.ds(0, FEAT)], local_sem.at[1]),
        pltpu.make_async_copy(wkv_in, wbuf.at[own_w, :, pl.ds(FEAT, HD)], local_sem.at[2]),
        pltpu.make_async_copy(og_in, og, local_sem.at[3]),
        pltpu.make_async_copy(cos_in, cos_ref, local_sem.at[4]),
        pltpu.make_async_copy(sin_in, sin_ref, local_sem.at[5]),
    ]
    for load in loads:
        load.start()
    pl.semaphore_wait(barrier, len(neighbours))

    def send_x(name, block, h, to):
        send((name, h), xs(block, h), xs(block, h), to)

    def recv_x(name, block, h):
        recv((name, h), xs(block, h))

    def send_w(name, block, h, to):
        send((name, h), ws(block, h), ws(block, h), to)

    def recv_w(name, block, h):
        recv((name, h), ws(block, h))

    def spread_y(j, h):
        send_x(("yp", j), tb(j, 0), h, yp)
        send_x(("ym", j), tb(j, 0), h, ym)

    loads[0].wait()
    for h in (0, 1):
        send_x("zp", own_x, h, zp)
        send_x("zm", own_x, 1 - h, zm)
        send_x(("yp", 0), own_x, h, yp)
        send_x(("ym", 0), own_x, 1 - h, ym)
    loads[1].wait()
    loads[2].wait()
    for h in (0, 1):
        send_w(("xp", 0), own_w, h, xp)
        send_w(("xm", 0), own_w, 1 - h, xm)
    for h in (0, 1):
        send_w("sib", own_w, h, sib)

    def relay_y(j, which):
        if which == 0:
            recv_x(("yp", j), tb(j, 3), 0)
            send_x(("ypr", j), tb(j, 3), 0, yp)
        else:
            recv_x(("ym", j), tb(j, 1), 1)
            send_x(("ymr", j), tb(j, 1), 1, ym)

    def relay_x(dz, which):
        if which == 0:
            recv_w(("xp", dz), wb(3, dz, 0), 0)
            send_w(("xpr", dz), wb(3, dz, 0), 0, xp)
            send_w(("sxp", dz), wb(3, dz, 0), 0, sib)
        else:
            recv_w(("xm", dz), wb(1, dz, 0), 1)
            send_w(("xmr", dz), wb(1, dz, 0), 1, xm)
            send_w(("sxm", dz), wb(1, dz, 0), 1, sib)

    def rest_x(dz):
        recv_w(("xp", dz), wb(3, dz, 0), 1)
        send_w(("sxp", dz), wb(3, dz, 0), 1, sib)
        recv_w(("xm", dz), wb(1, dz, 0), 0)
        send_w(("sxm", dz), wb(1, dz, 0), 0, sib)

    def far_x(dz):
        recv_w(("xpr", dz), wb(2, dz, 0), 0)
        send_w(("sfar", dz), wb(2, dz, 0), 0, sib)
        recv_w(("xmr", dz), wb(2, dz, 0), 1)
        send_w(("sfar", dz), wb(2, dz, 0), 1, sib)

    def from_zl(h):
        block = wb(0, 1, 0)
        recv_w("zl", block, h)
        send_w(("xp", 1), block, h, xp)
        send_w(("xm", 1), block, h, xm)
        send_w("szl", block, h, sib)

    acc[...] = jnp.zeros_like(acc)
    part[...] = jnp.zeros_like(part)
    for load in loads[3:]:
        load.wait()
    late = ((x + 2) % 4) * 2 + 1 - zl

    both, q_cols, kv_cols = slice(0, COLS), slice(0, FEAT), slice(FEAT, COLS)

    def project(b, ready, cols):
        @pl.when(ready)
        def _():
            acc[:, cols] += dot_nn(xbuf[b], wbuf[b, :, cols])

    def project_row(dh, dz, cols=both):
        first = ((zh + dh) % 4) * 4

        def one(i, carry):
            b = first + i
            same = (b // 2) % 2 == zl
            project(b, same if dz == 0 else jnp.logical_and(jnp.logical_not(same), b // 2 != late), cols)
            return carry

        lax.fori_loop(0, 4, one, 0)

    def rest_y(j):
        recv_x(("yp", j), tb(j, 3), 1)
        recv_x(("ym", j), tb(j, 1), 0)

    def far_y(j):
        recv_x(("ypr", j), tb(j, 2), 0)
        recv_x(("ymr", j), tb(j, 2), 1)

    relay_y(0, 0)
    relay_y(0, 1)
    relay_x(0, 0)
    relay_x(0, 1)
    recv_x("zp", tb(3, 0), 0)
    spread_y(3, 0)
    recv_x("zm", tb(1, 0), 1)
    spread_y(1, 1)
    send_w("zl", own_w, 0, zlp)
    rest_x(0)
    relay_y(3, 0)
    relay_y(1, 1)
    recv_x("zp", tb(3, 0), 1)
    spread_y(3, 1)
    recv_x("zm", tb(1, 0), 0)
    spread_y(1, 0)
    send_w("zl", own_w, 1, zlp)
    send_x("zpr", tb(3, 0), 0, zp)
    send_x("zmr", tb(1, 0), 1, zm)
    far_x(0)
    from_zl(0)
    relay_y(3, 1)
    relay_y(1, 0)
    from_zl(1)
    rest_y(0)
    far_y(0)
    for h in (0, 1):
        recv_w("sib", wb(0, 0, 1), h)
        recv_w(("sxp", 0), wb(3, 0, 1), h)
        recv_w(("sxm", 0), wb(1, 0, 1), h)
        recv_w(("sfar", 0), wb(2, 0, 1), h)
    recv_x("zpr", tb(2, 0), 0)
    spread_y(2, 0)
    recv_x("zmr", tb(2, 0), 1)
    spread_y(2, 1)
    project_row(0, 0)
    relay_x(1, 0)
    relay_x(1, 1)
    rest_y(3)
    far_y(3)
    project_row(3, 0)
    relay_y(2, 0)
    relay_y(2, 1)
    rest_y(1)
    far_y(1)
    project_row(1, 0)
    rest_x(1)
    for h in (0, 1):
        recv_w("szl", wb(0, 1, 1), h)
        recv_w(("sxp", 1), wb(3, 1, 1), h)
        recv_w(("sxm", 1), wb(1, 1, 1), h)
    project_row(0, 1)
    far_x(1)
    project_row(3, 1)
    project_row(1, 1)
    rest_y(2)
    far_y(2)
    project_row(2, 0, kv_cols)
    project_row(2, 1, kv_cols)
    for h in (0, 1):
        recv_w(("sfar", 1), wb(2, 1, 1), h)
    def last_two(cols):
        b0, b1 = wb(2, 1, 0), wb(2, 1, 1)
        acc[:, cols] += dot_nn(xbuf[b0], wbuf[b0, :, cols]) + dot_nn(xbuf[b1], wbuf[b1, :, cols])

    last_two(kv_cols)

    def rot(u, rows=slice(None)):
        return u * cos_ref[rows, :] + pltpu.roll(u, HD // 2, 1) * sin_ref[rows, :]

    def unrot(u, rows=slice(None)):
        return u * cos_ref[rows, :] - pltpu.roll(u, HD // 2, 1) * sin_ref[rows, :]

    raw = acc[:, FEAT:COLS]
    kv[role] = jnp.where(is_key, rot(raw), raw).astype(BF16)
    send("kv", kv.at[role], kv.at[role], mate)

    for i in range(8):
        send(("xsib", i), xbuf.at[2 * i + 1 - c], xsib.at[i], sib)

    project_row(2, 0, q_cols)
    project_row(2, 1, q_cols)
    last_two(q_cols)
    for h in range(HEADS):
        qbuf[:, h * HD:(h + 1) * HD] = rot(acc[:, h * HD:(h + 1) * HD]).astype(BF16)
    recv("kv", kv.at[1 - role])

    stores = []

    def store(src, dst):
        copy = pltpu.make_async_copy(src, dst, local_sem.at[len(loads) + len(stores)])
        copy.start()
        stores.append(copy)

    def t_rows(ch, h, j):
        first, size = CHUNKS[ch]
        if ch == 1 and j != 0:
            size -= LAST // 2
        return slice(first + h * size, first + (h + 1) * size)

    def t_part(ch, j):
        first, (_, size) = (0, HD)[ch], CHUNKS[ch]
        if ch == 1 and j != 0:
            size -= LAST // 2
        return slice(first, first + size)

    def g_rows(ch, h):
        return slice(ch * GC + h * GH, ch * GC + (h + 1) * GH)

    def g_part(ch):
        return slice(ch * GH, (ch + 1) * GH)

    def at(ref, i, rows):
        return ref.at[i, pl.ds(rows.start, rows.stop - rows.start)]

    def value(ref, i, rows):
        return ref[i, rows, :].astype(F32)

    def dx_half(j, dy, ch, h):
        mine = dot_nt(gbuf[t_rows(ch, h, j), :], wbuf[tb(j, dy)])
        if (j, ch, h) == (0, 1, 1):
            over_z = rq_full[0, dy].astype(F32) + rq_full[1, dy].astype(F32)
            mine = jnp.concatenate([mine[:-LAST], mine[-LAST:] + over_z], axis=0)
        return mine

    def last_rows(j):
        return [dot_nt(gbuf[MOST:, :], wbuf[tb(j, dy)]) for dy in range(4)]

    def put_last(name, j, values, part, dst, to):
        for dy in range(4):
            dxs[j * 4 + dy, MOST:, :] = values[dy].astype(BF16)
        send(name, dxs.at[pl.ds(j * 4, 4), pl.ds(MOST + part.start, part.stop - part.start)], dst, to)

    def q1():
        values, half = last_rows(2), LAST // 2
        put_last(("q1", 0), 2, values, slice(0, half), rq_half.at[0], zp)
        send(("q1", 1), dxs.at[pl.ds(8, 4), pl.ds(MOST + half, half)], rq_half.at[1], zm)

    def q2():
        half = LAST // 2
        for way, j, to in ((0, 1, zp), (1, 3, zm)):
            values = last_rows(j)
            recv(("q1", way), rq_half.at[way])
            for dy in range(4):
                first, second = values[dy][:half], values[dy][half:]
                if way == 0:
                    first = first + rq_half[0, dy].astype(F32)
                else:
                    second = second + rq_half[1, dy].astype(F32)
                values[dy] = jnp.concatenate([first, second], axis=0)
            put_last(("q2", way), j, values, slice(0, LAST), rq_full.at[way], to)

    def q3():
        for way in (0, 1):
            recv(("q2", way), rq_full.at[way])

    def dw_half(ddx, dz, ch, h):
        b, rows = wb(ddx, dz, 0), g_rows(ch, h)
        return dot_nn(gt[0, rows, :], xbuf[b]) + dot_nn(gt[1, rows, :], xsib[b // 2])

    def put_dx(name, j, dy, ch, h, mine, dst, to):
        i, rows = j * 4 + dy, t_rows(ch, h, j)
        dxs[i, rows, :] = mine.astype(BF16)
        send(name, at(dxs, i, rows), dst, to)

    def put_dw(name, ddx, dz, ch, h, mine, dst, to):
        i, rows = ddx * 2 + dz, g_rows(ch, h)
        dws[i, rows, :] = mine.astype(BF16)
        send(name, at(dws, i, rows), dst, to)

    def s1(ch, j0, j1):
        for h, j, to in ((0, j0, yp), (1, j1, ym)):
            put_dx(("s1", h, j, ch), j, 2, ch, h, dx_half(j, 2, ch, h), at(ry_half, j * 2 + h, t_part(ch, j)), to)

    def s2n(ch, j0, j1):
        for h, j, dy, way, to in ((1, j1, 1, 0, yp), (0, j0, 3, 1, ym)):
            dst = at(ry_full, j * 2 + way, t_rows(ch, h, j))
            put_dx(("s2", j, way, h, ch), j, dy, ch, h, dx_half(j, dy, ch, h), dst, to)

    def s2d(ch, j0, j1):
        for h, j, dy, to in ((0, j0, 1, yp), (1, j1, 3, ym)):
            mine = dx_half(j, dy, ch, h)
            recv(("s1", h, j, ch), at(ry_half, j * 2 + h, t_part(ch, j)))
            mine = mine + value(ry_half, j * 2 + h, t_part(ch, j))
            put_dx(("s2", j, h, h, ch), j, dy, ch, h, mine, at(ry_full, j * 2 + h, t_rows(ch, h, j)), to)

    def s3(ch, j0, j1):
        for h, j in ((0, j0), (1, j1)):
            rows = t_rows(ch, h, j)
            mine = dx_half(j, 0, ch, h)
            for way in (0, 1):
                recv(("s2", j, way, h, ch), at(ry_full, j * 2 + way, rows))
                mine = mine + value(ry_full, j * 2 + way, rows)
            if j == 2:
                put_dx(("z1", h, ch), j, 0, ch, h, mine, at(rz_half, h, t_part(ch, j)), zp if h == 0 else zm)
            elif j == 0:
                for way in (0, 1):
                    for part in ((h,) if ch == 0 else (0, 1) if h == 0 else ()):
                        recv(("z2", way, part, ch), at(rz_full, way, t_rows(ch, part, 1)))
                    if ch == 1 and h == 1:
                        over_z = value(rz_full, way, slice(rows.start, MOST))
                        mine = jnp.concatenate([mine[:-LAST] + over_z, mine[-LAST:]], axis=0)
                    else:
                        mine = mine + value(rz_full, way, rows)
                dx_st[rows, :] = mine.astype(BF16)
                part_rows = pl.ds(rows.start, rows.stop - rows.start)
                store(dx_st.at[part_rows], dx_out.at[part_rows])
            else:
                way = 0 if j == 1 else 1
                if h == way:
                    recv(("z1", h, ch), at(rz_half, h, t_part(ch, j)))
                    mine = mine + value(rz_half, h, t_part(ch, j))
                put_dx(("z2", way, h, ch), j, 0, ch, h, mine, at(rz_full, way, rows), zp if j == 1 else zm)

    def t1(dz, ch):
        for h, to in ((0, xp), (1, xm)):
            put_dw(("t1", h, dz, ch), 2, dz, ch, h, dw_half(2, dz, ch, h), at(rx_half, dz * 2 + h, g_part(ch)), to)

    def t2n(dz, ch):
        for h, ddx, way, to in ((1, 1, 0, xp), (0, 3, 1, xm)):
            dst = at(rx_full, dz * 2 + way, g_rows(ch, h))
            put_dw(("t2", dz, way, h, ch), ddx, dz, ch, h, dw_half(ddx, dz, ch, h), dst, to)

    def t2d(dz, ch):
        for h, ddx, to in ((0, 1, xp), (1, 3, xm)):
            mine = dw_half(ddx, dz, ch, h)
            recv(("t1", h, dz, ch), at(rx_half, dz * 2 + h, g_part(ch)))
            mine = mine + value(rx_half, dz * 2 + h, g_part(ch))
            put_dw(("t2", dz, h, h, ch), ddx, dz, ch, h, mine, at(rx_full, dz * 2 + h, g_rows(ch, h)), to)

    def t3(dz, ch):
        for h in (0, 1):
            rows = g_rows(ch, h)
            mine = dw_half(0, dz, ch, h)
            for way in (0, 1):
                recv(("t2", dz, way, h, ch), at(rx_full, dz * 2 + way, rows))
                mine = mine + value(rx_full, dz * 2 + way, rows)
            if dz == 1:
                put_dw(("t3", h, ch), 0, 1, ch, h, mine, at(rzl, 0, rows), zlp)
            else:
                recv(("t3", h, ch), at(rzl, 0, rows))
                t_st[rows, :] = mine + value(rzl, 0, rows)
                for k in range(rows.start // HD, rows.stop // HD):
                    block = t_st[k * HD:(k + 1) * HD, :].T.astype(BF16)
                    if k < HEADS:
                        qg_st[:, k * HD:(k + 1) * HD] = block
                        store(qg_st.at[:, pl.ds(k * HD, HD)], qg_out.at[:, pl.ds(k * HD, HD)])
                    else:
                        kvg_st[...] = block
                        store(kvg_st, kvg_out)

    scale = HD ** -0.5

    def finish_role(i):
        rows = slice(i * HD, (i + 1) * HD)
        recv(("part", i), part_in.at[pl.ds(i * HD, HD)])
        total = part[role, rows, :] + part_in[rows, :].astype(F32)
        total = jnp.where(is_key, unrot(total, rows), total)
        gbuf[rows, FEAT:COLS] = total.astype(BF16)
        gt[0, FEAT:COLS, rows] = total.T.astype(BF16)

    for i in reversed(range(TOK // HD)):
        rows, n = slice(i * HD, (i + 1) * HD), (i + 1) * HD

        def head(h, carry, i=i, rows=rows, n=n):
            cols = pl.ds(pl.multiple_of(h * HD, HD), HD)
            q, grad = qbuf[rows, cols], og[rows, cols]
            k, v = kv[0, :n], kv[1, :n]
            scores = dot_nt(q, k)
            q_pos = lax.broadcasted_iota(jnp.int32, (HD, n), 0) + i * HD
            k_pos = lax.broadcasted_iota(jnp.int32, (HD, n), 1)
            scores = jnp.where(k_pos <= q_pos, scores, -jnp.inf)
            expo = jnp.exp2((scores - jnp.max(scores, axis=-1, keepdims=True)) * (scale * LOG2E))
            probs = expo * (1.0 / jnp.sum(expo, axis=-1, keepdims=True))
            dprobs = dot_nt(grad, v)
            delta = jnp.sum(probs * dprobs, axis=-1, keepdims=True)
            dscores = (probs * ((dprobs - delta) * scale)).astype(BF16)
            dq = unrot(dot_nn(dscores, k), rows)
            gbuf[rows, cols] = dq.astype(BF16)
            gt[0, cols, rows] = dq.T.astype(BF16)
            part[0, :n] += dot_tn(dscores, q)
            part[1, :n] += dot_tn(probs.astype(BF16), grad)
            return carry

        lax.fori_loop(0, HEADS, head, 0, unroll=2 if i == 2 else 4)
        part_low[rows, :] = part[1 - role, rows, :].astype(BF16)
        send(("part", i), part_low.at[pl.ds(i * HD, HD)], part_in.at[pl.ds(i * HD, HD)], mate)
        if i == 1:
            finish_role(2)
            s1(1, 2, 2)
            s2n(1, 2, 2)
            s1(1, 3, 1)

    send("gt_q", gt.at[0, pl.ds(0, FEAT)], gt.at[1, pl.ds(0, FEAT)], sib)
    q1()
    s2d(1, 2, 2)
    for i in range(8):
        recv(("xsib", i), xsib.at[i])
    recv("gt_q", gt.at[1, pl.ds(0, FEAT)])
    t1(1, 0)
    t2n(1, 0)
    finish_role(1)
    finish_role(0)
    send("gt_kv", gt.at[0, pl.ds(FEAT, HD)], gt.at[1, pl.ds(FEAT, HD)], sib)
    s1(0, 2, 2)
    q2()
    s2n(1, 3, 1)
    s3(1, 2, 2)
    t2d(1, 0)
    s2n(0, 2, 2)
    recv("gt_kv", gt.at[1, pl.ds(FEAT, HD)])
    t1(1, 1)
    s2d(1, 3, 1)
    s1(1, 1, 3)
    t2n(1, 1)
    s2n(1, 1, 3)
    s2d(0, 2, 2)
    s1(0, 3, 1)
    s3(1, 3, 1)
    t3(1, 0)
    t2d(1, 1)
    t1(0, 0)
    s2d(1, 1, 3)
    s2n(0, 3, 1)
    s3(0, 2, 2)
    s2d(0, 3, 1)
    t2n(0, 0)
    s1(0, 1, 3)
    s2n(0, 1, 3)
    t2d(0, 0)
    t1(0, 1)
    s3(1, 1, 3)
    s3(0, 3, 1)
    t3(1, 1)
    s2d(0, 1, 3)
    t2n(0, 1)
    q3()
    s1(1, 0, 0)
    s2n(1, 0, 0)
    s1(0, 0, 0)
    s2n(0, 0, 0)
    t2d(0, 1)
    s2d(1, 0, 0)
    t3(0, 0)
    s3(0, 1, 3)
    s2d(0, 0, 0)
    s3(1, 0, 0)
    t3(0, 1)
    s3(0, 0, 0)

    for copy in stores:
        copy.wait()
    for copy in pending[-N_SEND:]:
        copy.wait_send()
    assert len(names) <= N_SEMS


def hand_on(*refs):
    n = len(refs) // 3
    sources, targets, held = refs[:n], refs[n:2 * n], refs[2 * n:3 * n]
    sem_in, sem_out = refs[3 * n:]
    steps = []
    for i in range(n):
        size = held[i].shape[0] // 2
        for h in (0, 1):
            k, rows = 2 * i + h, pl.ds(h * size, size)
            steps.append((
                pltpu.make_async_copy(sources[i].at[rows], held[i].at[rows], sem_in.at[k]),
                pltpu.make_async_copy(held[i].at[rows], targets[i].at[rows], sem_out.at[k]),
            ))
    for into, _ in steps:
        into.start()
    for into, out in steps:
        into.wait()
        out.start()
    for _, out in steps:
        out.wait()


def body(tokens_in, out_grad, q_weight, kv_weight):
    cosine, sine = rope_tables(TOK, HD)
    anywhere = pl.BlockSpec(memory_space=pl.ANY)
    outs = (
        jax.ShapeDtypeStruct((TOK, FEAT), BF16),
        jax.ShapeDtypeStruct((FEAT, FEAT), BF16),
        jax.ShapeDtypeStruct((FEAT, HD), BF16),
    )
    results = pl.pallas_call(
        kernel,
        out_shape=outs,
        in_specs=[anywhere] * 6,
        out_specs=(anywhere,) * 3,
        scratch_shapes=[
            pltpu.VMEM((TOK, HD), F32),
            pltpu.VMEM((TOK, HD), F32),
            pltpu.VMEM((TOK, FEAT), BF16),
            pltpu.VMEM((FEAT, FEAT), BF16),
            pltpu.VMEM((FEAT, HD), BF16),
            pltpu.VMEM((COLS, FEAT), F32),
            pltpu.VMEM((16, TOK, FEAT), BF16),
            pltpu.VMEM((16, FEAT, COLS), BF16),
            pltpu.VMEM((8, TOK, FEAT), BF16),
            pltpu.VMEM((TOK, FEAT), BF16),
            pltpu.VMEM((TOK, COLS), F32),
            pltpu.VMEM((TOK, FEAT), BF16),
            pltpu.VMEM((2, TOK, HD), BF16),
            pltpu.VMEM((TOK, COLS), BF16),
            pltpu.VMEM((2, COLS, TOK), BF16),
            pltpu.VMEM((2, TOK, HD), F32),
            pltpu.VMEM((TOK, HD), BF16),
            pltpu.VMEM((TOK, HD), BF16),
            pltpu.VMEM((16, TOK, FEAT), BF16),
            pltpu.VMEM((8, TOK, FEAT), BF16),
            pltpu.VMEM((8, HT, FEAT), BF16),
            pltpu.VMEM((2, TOK, FEAT), BF16),
            pltpu.VMEM((2, HT, FEAT), BF16),
            pltpu.VMEM((2, 4, LAST, FEAT), BF16),
            pltpu.VMEM((2, 4, LAST // 2, FEAT), BF16),
            pltpu.VMEM((8, COLS, FEAT), BF16),
            pltpu.VMEM((4, COLS, FEAT), BF16),
            pltpu.VMEM((4, GC, FEAT), BF16),
            pltpu.VMEM((1, COLS, FEAT), BF16),
            pltpu.SemaphoreType.DMA((16,)),
            pltpu.SemaphoreType.DMA((N_SEND,)),
            pltpu.SemaphoreType.DMA((N_SEMS,)),
        ],
        compiler_params=pltpu.CompilerParams(
            collective_id=0, has_side_effects=True, vmem_limit_bytes=60 * 2**20
        ),
        name="attention_backward",
    )(tokens_in, out_grad, q_weight, kv_weight, jnp.asarray(cosine), jnp.asarray(sine))
    return pl.pallas_call(
        hand_on,
        out_shape=outs,
        in_specs=[anywhere] * 3,
        out_specs=(anywhere,) * 3,
        scratch_shapes=[pltpu.VMEM(o.shape, o.dtype) for o in outs] + [pltpu.SemaphoreType.DMA((6,))] * 2,
        name="hand_on",
    )(*results)


def solution(mesh):
    spec = P("dp", "tensor")
    return jax.shard_map(
        body, mesh=mesh, in_specs=(spec,) * 4, out_specs=(spec,) * 3, check_vma=False
    )
```

```python
import functools
import jax
import jax.numpy as jnp
import numpy as np
from jax import lax
from jax.sharding import PartitionSpec as P
from jax.experimental import pallas as pl
from jax.experimental.pallas import tpu as pltpu

MESH = pl.DeviceIdType.MESH
F32, BF16 = jnp.float32, jnp.bfloat16
TOK, FEAT, HD, HEADS, COLS = 384, 512, 128, 4, 640
HT, HW = TOK // 2, FEAT // 2
GC, GH = COLS // 2, COLS // 4
CHUNKS = ((0, HD), (2 * HD, HD // 2))
LAST = 32
MOST = TOK - LAST
N_SEMS = 166
N_SEND = 56
LOG2E = float(np.log2(np.e))


def rope_tables(length, size):
    half = size // 2
    positions = np.arange(length, dtype=np.float32)
    inverse = np.power(
        np.float32(500000.0), -(np.arange(half, dtype=np.float32) * np.float32(2.0) / np.float32(size))
    ).astype(np.float32)
    angle = (positions[:, None] * inverse[None, :]).astype(np.float32).astype(np.float64)
    cosine, sine = np.cos(angle), np.sin(angle)
    return (
        np.concatenate([cosine, cosine], axis=1).astype(np.float32),
        np.concatenate([-sine, sine], axis=1).astype(np.float32),
    )


def dot_nn(a, b):
    return lax.dot_general(a, b, (((1,), (0,)), ((), ())), preferred_element_type=F32)


def dot_nt(a, b):
    return lax.dot_general(a, b, (((1,), (1,)), ((), ())), preferred_element_type=F32)


def dot_tn(a, b):
    return lax.dot_general(a, b, (((0,), (0,)), ((), ())), preferred_element_type=F32)


def kernel(
    x_in, og_in, wq_in, wkv_in, cos_in, sin_in,
    dx_out, qg_out, kvg_out,
    cos_ref, sin_ref, dx_st, qg_st, kvg_st, t_st,
    xbuf, wbuf, xsib, og, acc, qbuf, kv, gbuf, gt, part, part_low, part_in,
    dxs, ry_full, ry_half, rz_full, rz_half, rq_full, rq_half,
    dws, rx_full, rx_half, rzl,
    local_sem, ss, rs,
):
    dp, tn = lax.axis_index("dp"), lax.axis_index("tensor")
    x, zl, c = dp // 4, (dp // 2) % 2, dp % 2
    zh, y = tn // 4, tn % 4
    role = y % 2
    is_key = role == 0

    def wb(dx, dz, dc):
        return ((x + dx) % 4) * 4 + ((zl + dz) % 2) * 2 + (c + dc) % 2

    def tb(dh, dy):
        return ((zh + dh) % 4) * 4 + (y + dy) % 4

    sib = (wb(0, 0, 1), tn)
    zlp = (wb(0, 1, 0), tn)
    xp, xm = (wb(1, 0, 0), tn), (wb(3, 0, 0), tn)
    yp, ym = (dp, tb(0, 1)), (dp, tb(0, 3))
    zp, zm = (dp, tb(1, 0)), (dp, tb(3, 0))
    mate = (dp, zh * 4 + y + 1 - 2 * role)

    names = {}
    pending = []

    def sem(name):
        return names.setdefault(name, len(names))

    def send(name, src, dst, to):
        k, n = sem(name), len(pending)
        if n >= N_SEND:
            pending[n - N_SEND].wait_send()
        copy = pltpu.make_async_remote_copy(
            src_ref=src, dst_ref=dst, send_sem=ss.at[n % N_SEND], recv_sem=rs.at[k],
            device_id=to, device_id_type=MESH,
        )
        copy.start()
        pending.append(copy)

    def recv(name, dst):
        k = sem(name)
        pltpu.make_async_remote_copy(
            src_ref=dst, dst_ref=dst, send_sem=ss.at[0], recv_sem=rs.at[k],
            device_id=sib, device_id_type=MESH,
        ).wait_recv()

    def xs(block, h):
        return xbuf.at[block, pl.ds(h * HT, HT)]

    def ws(block, h):
        return wbuf.at[block, pl.ds(h * HW, HW)]

    own_x, own_w = tn, dp
    barrier = pltpu.get_barrier_semaphore()
    neighbours = (sib, zlp, xp, xm, yp, ym, zp, zm)
    for to in neighbours:
        pl.semaphore_signal(barrier, inc=1, device_id=to, device_id_type=MESH)
    loads = [
        pltpu.make_async_copy(x_in, xbuf.at[own_x], local_sem.at[0]),
        pltpu.make_async_copy(wq_in, wbuf.at[own_w, :, pl.ds(0, FEAT)], local_sem.at[1]),
        pltpu.make_async_copy(wkv_in, wbuf.at[own_w, :, pl.ds(FEAT, HD)], local_sem.at[2]),
        pltpu.make_async_copy(og_in, og, local_sem.at[3]),
        pltpu.make_async_copy(cos_in, cos_ref, local_sem.at[4]),
        pltpu.make_async_copy(sin_in, sin_ref, local_sem.at[5]),
    ]
    for load in loads:
        load.start()
    pl.semaphore_wait(barrier, len(neighbours))

    def send_x(name, block, h, to):
        send((name, h), xs(block, h), xs(block, h), to)

    def recv_x(name, block, h):
        recv((name, h), xs(block, h))

    def send_w(name, block, h, to):
        send((name, h), ws(block, h), ws(block, h), to)

    def recv_w(name, block, h):
        recv((name, h), ws(block, h))

    def spread_y(j, h):
        send_x(("yp", j), tb(j, 0), h, yp)
        send_x(("ym", j), tb(j, 0), h, ym)

    loads[0].wait()
    for h in (0, 1):
        send_x("zp", own_x, h, zp)
        send_x("zm", own_x, 1 - h, zm)
        send_x(("yp", 0), own_x, h, yp)
        send_x(("ym", 0), own_x, 1 - h, ym)
    loads[1].wait()
    loads[2].wait()
    for h in (0, 1):
        send_w(("xp", 0), own_w, h, xp)
        send_w(("xm", 0), own_w, 1 - h, xm)
    for h in (0, 1):
        send_w("sib", own_w, h, sib)

    def relay_y(j, which):
        if which == 0:
            recv_x(("yp", j), tb(j, 3), 0)
            send_x(("ypr", j), tb(j, 3), 0, yp)
        else:
            recv_x(("ym", j), tb(j, 1), 1)
            send_x(("ymr", j), tb(j, 1), 1, ym)

    def relay_x(dz, which):
        if which == 0:
            recv_w(("xp", dz), wb(3, dz, 0), 0)
            send_w(("xpr", dz), wb(3, dz, 0), 0, xp)
            send_w(("sxp", dz), wb(3, dz, 0), 0, sib)
        else:
            recv_w(("xm", dz), wb(1, dz, 0), 1)
            send_w(("xmr", dz), wb(1, dz, 0), 1, xm)
            send_w(("sxm", dz), wb(1, dz, 0), 1, sib)

    def rest_x(dz):
        recv_w(("xp", dz), wb(3, dz, 0), 1)
        send_w(("sxp", dz), wb(3, dz, 0), 1, sib)
        recv_w(("xm", dz), wb(1, dz, 0), 0)
        send_w(("sxm", dz), wb(1, dz, 0), 0, sib)

    def far_x(dz):
        recv_w(("xpr", dz), wb(2, dz, 0), 0)
        send_w(("sfar", dz), wb(2, dz, 0), 0, sib)
        recv_w(("xmr", dz), wb(2, dz, 0), 1)
        send_w(("sfar", dz), wb(2, dz, 0), 1, sib)

    def from_zl(h):
        block = wb(0, 1, 0)
        recv_w("zl", block, h)
        send_w(("xp", 1), block, h, xp)
        send_w(("xm", 1), block, h, xm)
        send_w("szl", block, h, sib)

    acc[...] = jnp.zeros_like(acc)
    part[...] = jnp.zeros_like(part)
    for load in loads[3:]:
        load.wait()
    late = ((x + 2) % 4) * 2 + 1 - zl

    both, q_cols, kv_cols = slice(0, COLS), slice(0, FEAT), slice(FEAT, COLS)

    def project(b, ready, cols):
        @pl.when(ready)
        def _():
            acc[:, cols] += dot_nn(xbuf[b], wbuf[b, :, cols])

    def project_row(dh, dz, cols=both):
        first = ((zh + dh) % 4) * 4

        def one(i, carry):
            b = first + i
            same = (b // 2) % 2 == zl
            project(b, same if dz == 0 else jnp.logical_and(jnp.logical_not(same), b // 2 != late), cols)
            return carry

        lax.fori_loop(0, 4, one, 0)

    def rest_y(j):
        recv_x(("yp", j), tb(j, 3), 1)
        recv_x(("ym", j), tb(j, 1), 0)

    def far_y(j):
        recv_x(("ypr", j), tb(j, 2), 0)
        recv_x(("ymr", j), tb(j, 2), 1)

    relay_y(0, 0)
    relay_y(0, 1)
    relay_x(0, 0)
    relay_x(0, 1)
    recv_x("zp", tb(3, 0), 0)
    spread_y(3, 0)
    recv_x("zm", tb(1, 0), 1)
    spread_y(1, 1)
    send_w("zl", own_w, 0, zlp)
    rest_x(0)
    relay_y(3, 0)
    relay_y(1, 1)
    recv_x("zp", tb(3, 0), 1)
    spread_y(3, 1)
    recv_x("zm", tb(1, 0), 0)
    spread_y(1, 0)
    send_w("zl", own_w, 1, zlp)
    send_x("zpr", tb(3, 0), 0, zp)
    send_x("zmr", tb(1, 0), 1, zm)
    far_x(0)
    from_zl(0)
    relay_y(3, 1)
    relay_y(1, 0)
    from_zl(1)
    rest_y(0)
    far_y(0)
    for h in (0, 1):
        recv_w("sib", wb(0, 0, 1), h)
        recv_w(("sxp", 0), wb(3, 0, 1), h)
        recv_w(("sxm", 0), wb(1, 0, 1), h)
        recv_w(("sfar", 0), wb(2, 0, 1), h)
    recv_x("zpr", tb(2, 0), 0)
    spread_y(2, 0)
    recv_x("zmr", tb(2, 0), 1)
    spread_y(2, 1)
    project_row(0, 0)
    relay_x(1, 0)
    relay_x(1, 1)
    rest_y(3)
    far_y(3)
    project_row(3, 0)
    relay_y(2, 0)
    relay_y(2, 1)
    rest_y(1)
    far_y(1)
    project_row(1, 0)
    rest_x(1)
    for h in (0, 1):
        recv_w("szl", wb(0, 1, 1), h)
        recv_w(("sxp", 1), wb(3, 1, 1), h)
        recv_w(("sxm", 1), wb(1, 1, 1), h)
    project_row(0, 1)
    far_x(1)
    project_row(3, 1)
    project_row(1, 1)
    rest_y(2)
    far_y(2)
    project_row(2, 0, kv_cols)
    project_row(2, 1, kv_cols)
    for h in (0, 1):
        recv_w(("sfar", 1), wb(2, 1, 1), h)
    def last_two(cols):
        b0, b1 = wb(2, 1, 0), wb(2, 1, 1)
        acc[:, cols] += dot_nn(xbuf[b0], wbuf[b0, :, cols]) + dot_nn(xbuf[b1], wbuf[b1, :, cols])

    last_two(kv_cols)

    def rot(u, rows=slice(None)):
        return u * cos_ref[rows, :] + pltpu.roll(u, HD // 2, 1) * sin_ref[rows, :]

    def unrot(u, rows=slice(None)):
        return u * cos_ref[rows, :] - pltpu.roll(u, HD // 2, 1) * sin_ref[rows, :]

    raw = acc[:, FEAT:COLS]
    kv[role] = jnp.where(is_key, rot(raw), raw).astype(BF16)
    send("kv", kv.at[role], kv.at[role], mate)

    for i in range(8):
        send(("xsib", i), xbuf.at[2 * i + 1 - c], xsib.at[i], sib)

    project_row(2, 0, q_cols)
    project_row(2, 1, q_cols)
    last_two(q_cols)
    for h in range(HEADS):
        qbuf[:, h * HD:(h + 1) * HD] = rot(acc[:, h * HD:(h + 1) * HD]).astype(BF16)
    recv("kv", kv.at[1 - role])

    stores = []

    def store(src, dst):
        copy = pltpu.make_async_copy(src, dst, local_sem.at[len(loads) + len(stores)])
        copy.start()
        stores.append(copy)

    def t_rows(ch, h, j):
        first, size = CHUNKS[ch]
        if ch == 1 and j != 0:
            size -= LAST // 2
        return slice(first + h * size, first + (h + 1) * size)

    def t_part(ch, j):
        first, (_, size) = (0, HD)[ch], CHUNKS[ch]
        if ch == 1 and j != 0:
            size -= LAST // 2
        return slice(first, first + size)

    def g_rows(ch, h):
        return slice(ch * GC + h * GH, ch * GC + (h + 1) * GH)

    def g_part(ch):
        return slice(ch * GH, (ch + 1) * GH)

    def at(ref, i, rows):
        return ref.at[i, pl.ds(rows.start, rows.stop - rows.start)]

    def value(ref, i, rows):
        return ref[i, rows, :].astype(F32)

    def dx_half(j, dy, ch, h):
        mine = dot_nt(gbuf[t_rows(ch, h, j), :], wbuf[tb(j, dy)])
        if (j, ch, h) == (0, 1, 1):
            over_z = rq_full[0, dy].astype(F32) + rq_full[1, dy].astype(F32)
            mine = jnp.concatenate([mine[:-LAST], mine[-LAST:] + over_z], axis=0)
        return mine

    def last_rows(j):
        return [dot_nt(gbuf[MOST:, :], wbuf[tb(j, dy)]) for dy in range(4)]

    def put_last(name, j, values, part, dst, to):
        for dy in range(4):
            dxs[j * 4 + dy, MOST:, :] = values[dy].astype(BF16)
        send(name, dxs.at[pl.ds(j * 4, 4), pl.ds(MOST + part.start, part.stop - part.start)], dst, to)

    def q1():
        values, half = last_rows(2), LAST // 2
        put_last(("q1", 0), 2, values, slice(0, half), rq_half.at[0], zp)
        send(("q1", 1), dxs.at[pl.ds(8, 4), pl.ds(MOST + half, half)], rq_half.at[1], zm)

    def q2():
        half = LAST // 2
        for way, j, to in ((0, 1, zp), (1, 3, zm)):
            values = last_rows(j)
            recv(("q1", way), rq_half.at[way])
            for dy in range(4):
                first, second = values[dy][:half], values[dy][half:]
                if way == 0:
                    first = first + rq_half[0, dy].astype(F32)
                else:
                    second = second + rq_half[1, dy].astype(F32)
                values[dy] = jnp.concatenate([first, second], axis=0)
            put_last(("q2", way), j, values, slice(0, LAST), rq_full.at[way], to)

    def q3():
        for way in (0, 1):
            recv(("q2", way), rq_full.at[way])

    def dw_half(ddx, dz, ch, h):
        b, rows = wb(ddx, dz, 0), g_rows(ch, h)
        return dot_nn(gt[0, rows, :], xbuf[b]) + dot_nn(gt[1, rows, :], xsib[b // 2])

    def put_dx(name, j, dy, ch, h, mine, dst, to):
        i, rows = j * 4 + dy, t_rows(ch, h, j)
        dxs[i, rows, :] = mine.astype(BF16)
        send(name, at(dxs, i, rows), dst, to)

    def put_dw(name, ddx, dz, ch, h, mine, dst, to):
        i, rows = ddx * 2 + dz, g_rows(ch, h)
        dws[i, rows, :] = mine.astype(BF16)
        send(name, at(dws, i, rows), dst, to)

    def s1(ch, j0, j1):
        for h, j, to in ((0, j0, yp), (1, j1, ym)):
            put_dx(("s1", h, j, ch), j, 2, ch, h, dx_half(j, 2, ch, h), at(ry_half, j * 2 + h, t_part(ch, j)), to)

    def s2n(ch, j0, j1):
        for h, j, dy, way, to in ((1, j1, 1, 0, yp), (0, j0, 3, 1, ym)):
            dst = at(ry_full, j * 2 + way, t_rows(ch, h, j))
            put_dx(("s2", j, way, h, ch), j, dy, ch, h, dx_half(j, dy, ch, h), dst, to)

    def s2d(ch, j0, j1):
        for h, j, dy, to in ((0, j0, 1, yp), (1, j1, 3, ym)):
            mine = dx_half(j, dy, ch, h)
            recv(("s1", h, j, ch), at(ry_half, j * 2 + h, t_part(ch, j)))
            mine = mine + value(ry_half, j * 2 + h, t_part(ch, j))
            put_dx(("s2", j, h, h, ch), j, dy, ch, h, mine, at(ry_full, j * 2 + h, t_rows(ch, h, j)), to)

    def s3(ch, j0, j1):
        for h, j in ((0, j0), (1, j1)):
            rows = t_rows(ch, h, j)
            mine = dx_half(j, 0, ch, h)
            for way in (0, 1):
                recv(("s2", j, way, h, ch), at(ry_full, j * 2 + way, rows))
                mine = mine + value(ry_full, j * 2 + way, rows)
            if j == 2:
                put_dx(("z1", h, ch), j, 0, ch, h, mine, at(rz_half, h, t_part(ch, j)), zp if h == 0 else zm)
            elif j == 0:
                for way in (0, 1):
                    for part in ((h,) if ch == 0 else (0, 1) if h == 0 else ()):
                        recv(("z2", way, part, ch), at(rz_full, way, t_rows(ch, part, 1)))
                    if ch == 1 and h == 1:
                        over_z = value(rz_full, way, slice(rows.start, MOST))
                        mine = jnp.concatenate([mine[:-LAST] + over_z, mine[-LAST:]], axis=0)
                    else:
                        mine = mine + value(rz_full, way, rows)
                dx_st[rows, :] = mine.astype(BF16)
                part_rows = pl.ds(rows.start, rows.stop - rows.start)
                store(dx_st.at[part_rows], dx_out.at[part_rows])
            else:
                way = 0 if j == 1 else 1
                if h == way:
                    recv(("z1", h, ch), at(rz_half, h, t_part(ch, j)))
                    mine = mine + value(rz_half, h, t_part(ch, j))
                put_dx(("z2", way, h, ch), j, 0, ch, h, mine, at(rz_full, way, rows), zp if j == 1 else zm)

    def t1(dz, ch):
        for h, to in ((0, xp), (1, xm)):
            put_dw(("t1", h, dz, ch), 2, dz, ch, h, dw_half(2, dz, ch, h), at(rx_half, dz * 2 + h, g_part(ch)), to)

    def t2n(dz, ch):
        for h, ddx, way, to in ((1, 1, 0, xp), (0, 3, 1, xm)):
            dst = at(rx_full, dz * 2 + way, g_rows(ch, h))
            put_dw(("t2", dz, way, h, ch), ddx, dz, ch, h, dw_half(ddx, dz, ch, h), dst, to)

    def t2d(dz, ch):
        for h, ddx, to in ((0, 1, xp), (1, 3, xm)):
            mine = dw_half(ddx, dz, ch, h)
            recv(("t1", h, dz, ch), at(rx_half, dz * 2 + h, g_part(ch)))
            mine = mine + value(rx_half, dz * 2 + h, g_part(ch))
            put_dw(("t2", dz, h, h, ch), ddx, dz, ch, h, mine, at(rx_full, dz * 2 + h, g_rows(ch, h)), to)

    def t3(dz, ch):
        for h in (0, 1):
            rows = g_rows(ch, h)
            mine = dw_half(0, dz, ch, h)
            for way in (0, 1):
                recv(("t2", dz, way, h, ch), at(rx_full, dz * 2 + way, rows))
                mine = mine + value(rx_full, dz * 2 + way, rows)
            if dz == 1:
                put_dw(("t3", h, ch), 0, 1, ch, h, mine, at(rzl, 0, rows), zlp)
            else:
                recv(("t3", h, ch), at(rzl, 0, rows))
                t_st[rows, :] = mine + value(rzl, 0, rows)
                for k in range(rows.start // HD, rows.stop // HD):
                    block = t_st[k * HD:(k + 1) * HD, :].T.astype(BF16)
                    if k < HEADS:
                        qg_st[:, k * HD:(k + 1) * HD] = block
                        store(qg_st.at[:, pl.ds(k * HD, HD)], qg_out.at[:, pl.ds(k * HD, HD)])
                    else:
                        kvg_st[...] = block
                        store(kvg_st, kvg_out)

    scale = HD ** -0.5

    def finish_role(i):
        rows = slice(i * HD, (i + 1) * HD)
        recv(("part", i), part_in.at[pl.ds(i * HD, HD)])
        total = part[role, rows, :] + part_in[rows, :].astype(F32)
        total = jnp.where(is_key, unrot(total, rows), total)
        gbuf[rows, FEAT:COLS] = total.astype(BF16)
        gt[0, FEAT:COLS, rows] = total.T.astype(BF16)

    for i in reversed(range(TOK // HD)):
        rows, n = slice(i * HD, (i + 1) * HD), (i + 1) * HD

        def head(h, carry, i=i, rows=rows, n=n):
            cols = pl.ds(pl.multiple_of(h * HD, HD), HD)
            q, grad = qbuf[rows, cols], og[rows, cols]
            k, v = kv[0, :n], kv[1, :n]
            scores = dot_nt(q, k)
            q_pos = lax.broadcasted_iota(jnp.int32, (HD, HD), 0)
            k_pos = lax.broadcasted_iota(jnp.int32, (HD, HD), 1)
            last = jnp.where(k_pos <= q_pos, scores[:, n - HD:], -jnp.inf)
            scores = last if i == 0 else jnp.concatenate([scores[:, :n - HD], last], axis=1)
            expo = jnp.exp2((scores - jnp.max(scores, axis=-1, keepdims=True)) * (scale * LOG2E))
            probs = expo * (1.0 / jnp.sum(expo, axis=-1, keepdims=True))
            dprobs = dot_nt(grad, v)
            delta = jnp.sum(probs * dprobs, axis=-1, keepdims=True)
            dscores = (probs * ((dprobs - delta) * scale)).astype(BF16)
            dq = unrot(dot_nn(dscores, k), rows)
            gbuf[rows, cols] = dq.astype(BF16)
            gt[0, cols, rows] = dq.T.astype(BF16)
            part[0, :n] += dot_tn(dscores, q)
            part[1, :n] += dot_tn(probs.astype(BF16), grad)
            return carry

        lax.fori_loop(0, HEADS, head, 0, unroll=4)
        part_low[rows, :] = part[1 - role, rows, :].astype(BF16)
        send(("part", i), part_low.at[pl.ds(i * HD, HD)], part_in.at[pl.ds(i * HD, HD)], mate)
        if i == 1:
            finish_role(2)
            s1(1, 2, 2)
            s2n(1, 2, 2)
            s1(1, 3, 1)

    send("gt_q", gt.at[0, pl.ds(0, FEAT)], gt.at[1, pl.ds(0, FEAT)], sib)
    q1()
    s2d(1, 2, 2)
    for i in range(8):
        recv(("xsib", i), xsib.at[i])
    recv("gt_q", gt.at[1, pl.ds(0, FEAT)])
    t1(1, 0)
    t2n(1, 0)
    finish_role(1)
    finish_role(0)
    send("gt_kv", gt.at[0, pl.ds(FEAT, HD)], gt.at[1, pl.ds(FEAT, HD)], sib)
    s1(0, 2, 2)
    q2()
    s2n(1, 3, 1)
    s3(1, 2, 2)
    t2d(1, 0)
    s2n(0, 2, 2)
    recv("gt_kv", gt.at[1, pl.ds(FEAT, HD)])
    t1(1, 1)
    s2d(1, 3, 1)
    s1(1, 1, 3)
    t2n(1, 1)
    s2n(1, 1, 3)
    s2d(0, 2, 2)
    s1(0, 3, 1)
    s3(1, 3, 1)
    t3(1, 0)
    t2d(1, 1)
    t1(0, 0)
    s2d(1, 1, 3)
    s2n(0, 3, 1)
    s3(0, 2, 2)
    s2d(0, 3, 1)
    t2n(0, 0)
    s1(0, 1, 3)
    s2n(0, 1, 3)
    t2d(0, 0)
    t1(0, 1)
    s3(1, 1, 3)
    s3(0, 3, 1)
    t3(1, 1)
    s2d(0, 1, 3)
    t2n(0, 1)
    q3()
    s1(1, 0, 0)
    s2n(1, 0, 0)
    s1(0, 0, 0)
    s2n(0, 0, 0)
    t2d(0, 1)
    s2d(1, 0, 0)
    t3(0, 0)
    s3(0, 1, 3)
    s2d(0, 0, 0)
    s3(1, 0, 0)
    t3(0, 1)
    s3(0, 0, 0)

    for copy in stores:
        copy.wait()
    for copy in pending[-N_SEND:]:
        copy.wait_send()
    assert len(names) <= N_SEMS


def hand_on(*refs):
    n = len(refs) // 3
    sources, targets, held = refs[:n], refs[n:2 * n], refs[2 * n:3 * n]
    sem_in, sem_out = refs[3 * n:]
    steps = []
    for i in range(n):
        size = held[i].shape[0] // 2
        for h in (0, 1):
            k, rows = 2 * i + h, pl.ds(h * size, size)
            steps.append((
                pltpu.make_async_copy(sources[i].at[rows], held[i].at[rows], sem_in.at[k]),
                pltpu.make_async_copy(held[i].at[rows], targets[i].at[rows], sem_out.at[k]),
            ))
    for into, _ in steps:
        into.start()
    for into, out in steps:
        into.wait()
        out.start()
    for _, out in steps:
        out.wait()


def body(tokens_in, out_grad, q_weight, kv_weight):
    cosine, sine = rope_tables(TOK, HD)
    anywhere = pl.BlockSpec(memory_space=pl.ANY)
    outs = (
        jax.ShapeDtypeStruct((TOK, FEAT), BF16),
        jax.ShapeDtypeStruct((FEAT, FEAT), BF16),
        jax.ShapeDtypeStruct((FEAT, HD), BF16),
    )
    results = pl.pallas_call(
        kernel,
        out_shape=outs,
        in_specs=[anywhere] * 6,
        out_specs=(anywhere,) * 3,
        scratch_shapes=[
            pltpu.VMEM((TOK, HD), F32),
            pltpu.VMEM((TOK, HD), F32),
            pltpu.VMEM((TOK, FEAT), BF16),
            pltpu.VMEM((FEAT, FEAT), BF16),
            pltpu.VMEM((FEAT, HD), BF16),
            pltpu.VMEM((COLS, FEAT), F32),
            pltpu.VMEM((16, TOK, FEAT), BF16),
            pltpu.VMEM((16, FEAT, COLS), BF16),
            pltpu.VMEM((8, TOK, FEAT), BF16),
            pltpu.VMEM((TOK, FEAT), BF16),
            pltpu.VMEM((TOK, COLS), F32),
            pltpu.VMEM((TOK, FEAT), BF16),
            pltpu.VMEM((2, TOK, HD), BF16),
            pltpu.VMEM((TOK, COLS), BF16),
            pltpu.VMEM((2, COLS, TOK), BF16),
            pltpu.VMEM((2, TOK, HD), F32),
            pltpu.VMEM((TOK, HD), BF16),
            pltpu.VMEM((TOK, HD), BF16),
            pltpu.VMEM((16, TOK, FEAT), BF16),
            pltpu.VMEM((8, TOK, FEAT), BF16),
            pltpu.VMEM((8, HT, FEAT), BF16),
            pltpu.VMEM((2, TOK, FEAT), BF16),
            pltpu.VMEM((2, HT, FEAT), BF16),
            pltpu.VMEM((2, 4, LAST, FEAT), BF16),
            pltpu.VMEM((2, 4, LAST // 2, FEAT), BF16),
            pltpu.VMEM((8, COLS, FEAT), BF16),
            pltpu.VMEM((4, COLS, FEAT), BF16),
            pltpu.VMEM((4, GC, FEAT), BF16),
            pltpu.VMEM((1, COLS, FEAT), BF16),
            pltpu.SemaphoreType.DMA((16,)),
            pltpu.SemaphoreType.DMA((N_SEND,)),
            pltpu.SemaphoreType.DMA((N_SEMS,)),
        ],
        compiler_params=pltpu.CompilerParams(
            collective_id=0, has_side_effects=True, vmem_limit_bytes=60 * 2**20
        ),
        name="attention_backward",
    )(tokens_in, out_grad, q_weight, kv_weight, jnp.asarray(cosine), jnp.asarray(sine))
    return pl.pallas_call(
        hand_on,
        out_shape=outs,
        in_specs=[anywhere] * 3,
        out_specs=(anywhere,) * 3,
        scratch_shapes=[pltpu.VMEM(o.shape, o.dtype) for o in outs] + [pltpu.SemaphoreType.DMA((6,))] * 2,
        name="hand_on",
    )(*results)


def solution(mesh):
    spec = P("dp", "tensor")
    return jax.shard_map(
        body, mesh=mesh, in_specs=(spec,) * 4, out_specs=(spec,) * 3, check_vma=False
    )
```

```python
import functools
import jax
import jax.numpy as jnp
import numpy as np
from jax import lax
from jax.sharding import PartitionSpec as P
from jax.experimental import pallas as pl
from jax.experimental.pallas import tpu as pltpu

MESH = pl.DeviceIdType.MESH
F32, BF16 = jnp.float32, jnp.bfloat16
TOK, FEAT, HD, HEADS, COLS = 384, 512, 128, 4, 640
HT, HW = TOK // 2, FEAT // 2
GC, GH = COLS // 2, COLS // 4
CHUNKS = ((0, HD), (2 * HD, HD // 2))
LAST = 32
MOST = TOK - LAST
N_SEMS = 178
N_SEND = 56
LOG2E = float(np.log2(np.e))


def rope_tables(length, size):
    half = size // 2
    positions = np.arange(length, dtype=np.float32)
    inverse = np.power(
        np.float32(500000.0), -(np.arange(half, dtype=np.float32) * np.float32(2.0) / np.float32(size))
    ).astype(np.float32)
    angle = (positions[:, None] * inverse[None, :]).astype(np.float32).astype(np.float64)
    cosine, sine = np.cos(angle), np.sin(angle)
    return (
        np.concatenate([cosine, cosine], axis=1).astype(np.float32),
        np.concatenate([-sine, sine], axis=1).astype(np.float32),
    )


def dot_nn(a, b):
    return lax.dot_general(a, b, (((1,), (0,)), ((), ())), preferred_element_type=F32)


def dot_nt(a, b):
    return lax.dot_general(a, b, (((1,), (1,)), ((), ())), preferred_element_type=F32)


def dot_tn(a, b):
    return lax.dot_general(a, b, (((0,), (0,)), ((), ())), preferred_element_type=F32)


def kernel(
    x_in, og_in, wq_in, wkv_in, cos_in, sin_in,
    dx_out, qg_out, kvg_out,
    cos_ref, sin_ref, dx_st, qg_st, kvg_st, t_st,
    xbuf, wbuf, xsib, og, acc, qbuf, kv, gbuf, gt, part, part_low, part_in,
    dxs, ry_full, ry_half, rz_full, rz_half, rq_full, rq_half,
    dws, rx_full, rx_half, rzl,
    local_sem, ss, rs,
):
    dp, tn = lax.axis_index("dp"), lax.axis_index("tensor")
    x, zl, c = dp // 4, (dp // 2) % 2, dp % 2
    zh, y = tn // 4, tn % 4
    role = y % 2
    is_key = role == 0

    def wb(dx, dz, dc):
        return ((x + dx) % 4) * 4 + ((zl + dz) % 2) * 2 + (c + dc) % 2

    def tb(dh, dy):
        return ((zh + dh) % 4) * 4 + (y + dy) % 4

    sib = (wb(0, 0, 1), tn)
    zlp = (wb(0, 1, 0), tn)
    xp, xm = (wb(1, 0, 0), tn), (wb(3, 0, 0), tn)
    yp, ym = (dp, tb(0, 1)), (dp, tb(0, 3))
    zp, zm = (dp, tb(1, 0)), (dp, tb(3, 0))
    mate = (dp, zh * 4 + y + 1 - 2 * role)

    names = {}
    pending = []

    def sem(name):
        return names.setdefault(name, len(names))

    def send(name, src, dst, to):
        k, n = sem(name), len(pending)
        if n >= N_SEND:
            pending[n - N_SEND].wait_send()
        copy = pltpu.make_async_remote_copy(
            src_ref=src, dst_ref=dst, send_sem=ss.at[n % N_SEND], recv_sem=rs.at[k],
            device_id=to, device_id_type=MESH,
        )
        copy.start()
        pending.append(copy)

    def recv(name, dst):
        k = sem(name)
        pltpu.make_async_remote_copy(
            src_ref=dst, dst_ref=dst, send_sem=ss.at[0], recv_sem=rs.at[k],
            device_id=sib, device_id_type=MESH,
        ).wait_recv()

    def xs(block, h):
        return xbuf.at[block, pl.ds(h * HT, HT)]

    def ws(block, h):
        return wbuf.at[block, pl.ds(h * HW, HW)]

    own_x, own_w = tn, dp
    barrier = pltpu.get_barrier_semaphore()
    neighbours = (sib, zlp, xp, xm, yp, ym, zp, zm)
    for to in neighbours:
        pl.semaphore_signal(barrier, inc=1, device_id=to, device_id_type=MESH)
    loads = [
        pltpu.make_async_copy(x_in, xbuf.at[own_x], local_sem.at[0]),
        pltpu.make_async_copy(wq_in, wbuf.at[own_w, :, pl.ds(0, FEAT)], local_sem.at[1]),
        pltpu.make_async_copy(wkv_in, wbuf.at[own_w, :, pl.ds(FEAT, HD)], local_sem.at[2]),
        pltpu.make_async_copy(og_in, og, local_sem.at[3]),
        pltpu.make_async_copy(cos_in, cos_ref, local_sem.at[4]),
        pltpu.make_async_copy(sin_in, sin_ref, local_sem.at[5]),
    ]
    for load in loads:
        load.start()
    pl.semaphore_wait(barrier, len(neighbours))

    def send_x(name, block, h, to):
        send((name, h), xs(block, h), xs(block, h), to)

    def recv_x(name, block, h):
        recv((name, h), xs(block, h))

    def send_w(name, block, h, to):
        send((name, h), ws(block, h), ws(block, h), to)

    def recv_w(name, block, h):
        recv((name, h), ws(block, h))

    def spread_y(j, h):
        send_x(("yp", j), tb(j, 0), h, yp)
        send_x(("ym", j), tb(j, 0), h, ym)

    loads[0].wait()
    for h in (0, 1):
        send_x("zp", own_x, h, zp)
        send_x("zm", own_x, 1 - h, zm)
        send_x(("yp", 0), own_x, h, yp)
        send_x(("ym", 0), own_x, 1 - h, ym)
    loads[1].wait()
    loads[2].wait()
    for h in (0, 1):
        send_w(("xp", 0), own_w, h, xp)
        send_w(("xm", 0), own_w, 1 - h, xm)
    for h in (0, 1):
        send_w("sib", own_w, h, sib)

    def relay_y(j, which):
        if which == 0:
            recv_x(("yp", j), tb(j, 3), 0)
            send_x(("ypr", j), tb(j, 3), 0, yp)
        else:
            recv_x(("ym", j), tb(j, 1), 1)
            send_x(("ymr", j), tb(j, 1), 1, ym)

    def relay_x(dz, which):
        if which == 0:
            recv_w(("xp", dz), wb(3, dz, 0), 0)
            send_w(("xpr", dz), wb(3, dz, 0), 0, xp)
            send_w(("sxp", dz), wb(3, dz, 0), 0, sib)
        else:
            recv_w(("xm", dz), wb(1, dz, 0), 1)
            send_w(("xmr", dz), wb(1, dz, 0), 1, xm)
            send_w(("sxm", dz), wb(1, dz, 0), 1, sib)

    def rest_x(dz):
        recv_w(("xp", dz), wb(3, dz, 0), 1)
        send_w(("sxp", dz), wb(3, dz, 0), 1, sib)
        recv_w(("xm", dz), wb(1, dz, 0), 0)
        send_w(("sxm", dz), wb(1, dz, 0), 0, sib)

    def far_x(dz):
        recv_w(("xpr", dz), wb(2, dz, 0), 0)
        send_w(("sfar", dz), wb(2, dz, 0), 0, sib)
        recv_w(("xmr", dz), wb(2, dz, 0), 1)
        send_w(("sfar", dz), wb(2, dz, 0), 1, sib)

    def quarter(block, p):
        return wbuf.at[block, pl.ds(p * (HW // 2), HW // 2)]

    def send_q(name, block, p, to):
        send((name, p), quarter(block, p), quarter(block, p), to)

    def recv_q(name, block, p):
        recv((name, p), quarter(block, p))

    def from_zl(h):
        block = wb(0, 1, 0)
        recv_w("zl", block, h)
        for k in (0, 1):
            send_q("xpq", block, 2 * h + k, xp)
            send_q("xmq", block, 2 * h + 1 - k, xm)
        send_w("szl", block, h, sib)

    def relay_q(h):
        recv_q("xpq", wb(3, 1, 0), 2 * h)
        send_q("xpqr", wb(3, 1, 0), 2 * h, xp)
        recv_q("xmq", wb(1, 1, 0), 2 * h + 1)
        send_q("xmqr", wb(1, 1, 0), 2 * h + 1, xm)
        send_q("sxpq", wb(3, 1, 0), 2 * h, sib)
        send_q("sxmq", wb(1, 1, 0), 2 * h + 1, sib)

    def rest_q(h):
        recv_q("xpq", wb(3, 1, 0), 2 * h + 1)
        send_q("sxpq", wb(3, 1, 0), 2 * h + 1, sib)
        recv_q("xmq", wb(1, 1, 0), 2 * h)
        send_q("sxmq", wb(1, 1, 0), 2 * h, sib)

    def far_q(h):
        recv_q("xpqr", wb(2, 1, 0), 2 * h)
        send_q("sfarq", wb(2, 1, 0), 2 * h, sib)
        recv_q("xmqr", wb(2, 1, 0), 2 * h + 1)
        send_q("sfarq", wb(2, 1, 0), 2 * h + 1, sib)

    acc[...] = jnp.zeros_like(acc)
    part[...] = jnp.zeros_like(part)
    for load in loads[3:]:
        load.wait()
    late = ((x + 2) % 4) * 2 + 1 - zl

    both, q_cols, kv_cols = slice(0, COLS), slice(0, FEAT), slice(FEAT, COLS)

    def project(b, ready, cols):
        @pl.when(ready)
        def _():
            acc[:, cols] += dot_nn(xbuf[b], wbuf[b, :, cols])

    def project_row(dh, dz, cols=both):
        first = ((zh + dh) % 4) * 4

        def one(i, carry):
            b = first + i
            same = (b // 2) % 2 == zl
            project(b, same if dz == 0 else jnp.logical_and(jnp.logical_not(same), b // 2 != late), cols)
            return carry

        lax.fori_loop(0, 4, one, 0)

    def rest_y(j):
        recv_x(("yp", j), tb(j, 3), 1)
        recv_x(("ym", j), tb(j, 1), 0)

    def far_y(j):
        recv_x(("ypr", j), tb(j, 2), 0)
        recv_x(("ymr", j), tb(j, 2), 1)

    relay_y(0, 0)
    relay_y(0, 1)
    relay_x(0, 0)
    relay_x(0, 1)
    recv_x("zp", tb(3, 0), 0)
    spread_y(3, 0)
    recv_x("zm", tb(1, 0), 1)
    spread_y(1, 1)
    send_w("zl", own_w, 0, zlp)
    rest_x(0)
    relay_y(3, 0)
    relay_y(1, 1)
    recv_x("zp", tb(3, 0), 1)
    spread_y(3, 1)
    recv_x("zm", tb(1, 0), 0)
    spread_y(1, 0)
    send_w("zl", own_w, 1, zlp)
    send_x("zpr", tb(3, 0), 0, zp)
    send_x("zmr", tb(1, 0), 1, zm)
    far_x(0)
    from_zl(0)
    relay_y(3, 1)
    relay_q(0)
    relay_y(1, 0)
    from_zl(1)
    rest_y(0)
    far_y(0)
    for h in (0, 1):
        recv_w("sib", wb(0, 0, 1), h)
        recv_w(("sxp", 0), wb(3, 0, 1), h)
        recv_w(("sxm", 0), wb(1, 0, 1), h)
        recv_w(("sfar", 0), wb(2, 0, 1), h)
    recv_x("zpr", tb(2, 0), 0)
    spread_y(2, 0)
    recv_x("zmr", tb(2, 0), 1)
    spread_y(2, 1)
    rest_q(0)
    far_q(0)
    project_row(0, 0)
    rest_y(3)
    far_y(3)
    project_row(3, 0)
    relay_q(1)
    relay_y(2, 0)
    relay_y(2, 1)
    rest_y(1)
    far_y(1)
    project_row(1, 0)
    rest_q(1)
    for h in (0, 1):
        recv_w("szl", wb(0, 1, 1), h)
        for p in (2 * h, 2 * h + 1):
            recv_q("sxpq", wb(3, 1, 1), p)
            recv_q("sxmq", wb(1, 1, 1), p)
    project_row(0, 1)
    far_q(1)
    project_row(3, 1)
    project_row(1, 1)
    rest_y(2)
    far_y(2)
    project_row(2, 0, kv_cols)
    project_row(2, 1, kv_cols)
    for p in range(4):
        recv_q("sfarq", wb(2, 1, 1), p)
    def last_two(cols):
        b0, b1 = wb(2, 1, 0), wb(2, 1, 1)
        acc[:, cols] += dot_nn(xbuf[b0], wbuf[b0, :, cols]) + dot_nn(xbuf[b1], wbuf[b1, :, cols])

    last_two(kv_cols)

    def rot(u, rows=slice(None)):
        return u * cos_ref[rows, :] + pltpu.roll(u, HD // 2, 1) * sin_ref[rows, :]

    def unrot(u, rows=slice(None)):
        return u * cos_ref[rows, :] - pltpu.roll(u, HD // 2, 1) * sin_ref[rows, :]

    raw = acc[:, FEAT:COLS]
    kv[role] = jnp.where(is_key, rot(raw), raw).astype(BF16)
    send("kv", kv.at[role], kv.at[role], mate)

    for i in range(8):
        send(("xsib", i), xbuf.at[2 * i + 1 - c], xsib.at[i], sib)

    project_row(2, 0, q_cols)
    project_row(2, 1, q_cols)
    last_two(q_cols)
    for h in range(HEADS):
        qbuf[:, h * HD:(h + 1) * HD] = rot(acc[:, h * HD:(h + 1) * HD]).astype(BF16)
    recv("kv", kv.at[1 - role])

    stores = []

    def store(src, dst):
        copy = pltpu.make_async_copy(src, dst, local_sem.at[len(loads) + len(stores)])
        copy.start()
        stores.append(copy)

    def t_rows(ch, h, j):
        first, size = CHUNKS[ch]
        if ch == 1 and j != 0:
            size -= LAST // 2
        return slice(first + h * size, first + (h + 1) * size)

    def t_part(ch, j):
        first, (_, size) = (0, HD)[ch], CHUNKS[ch]
        if ch == 1 and j != 0:
            size -= LAST // 2
        return slice(first, first + size)

    def g_rows(ch, h):
        return slice(ch * GC + h * GH, ch * GC + (h + 1) * GH)

    def g_part(ch):
        return slice(ch * GH, (ch + 1) * GH)

    def at(ref, i, rows):
        return ref.at[i, pl.ds(rows.start, rows.stop - rows.start)]

    def value(ref, i, rows):
        return ref[i, rows, :].astype(F32)

    def dx_half(j, dy, ch, h):
        mine = dot_nt(gbuf[t_rows(ch, h, j), :], wbuf[tb(j, dy)])
        if (j, ch, h) == (0, 1, 1):
            over_z = rq_full[0, dy].astype(F32) + rq_full[1, dy].astype(F32)
            mine = jnp.concatenate([mine[:-LAST], mine[-LAST:] + over_z], axis=0)
        return mine

    def last_rows(j):
        return [dot_nt(gbuf[MOST:, :], wbuf[tb(j, dy)]) for dy in range(4)]

    def put_last(name, j, values, part, dst, to):
        for dy in range(4):
            dxs[j * 4 + dy, MOST:, :] = values[dy].astype(BF16)
        send(name, dxs.at[pl.ds(j * 4, 4), pl.ds(MOST + part.start, part.stop - part.start)], dst, to)

    def q1():
        values, half = last_rows(2), LAST // 2
        put_last(("q1", 0), 2, values, slice(0, half), rq_half.at[0], zp)
        send(("q1", 1), dxs.at[pl.ds(8, 4), pl.ds(MOST + half, half)], rq_half.at[1], zm)

    def q2():
        half = LAST // 2
        for way, j, to in ((0, 1, zp), (1, 3, zm)):
            values = last_rows(j)
            recv(("q1", way), rq_half.at[way])
            for dy in range(4):
                first, second = values[dy][:half], values[dy][half:]
                if way == 0:
                    first = first + rq_half[0, dy].astype(F32)
                else:
                    second = second + rq_half[1, dy].astype(F32)
                values[dy] = jnp.concatenate([first, second], axis=0)
            put_last(("q2", way), j, values, slice(0, LAST), rq_full.at[way], to)

    def q3():
        for way in (0, 1):
            recv(("q2", way), rq_full.at[way])

    def dw_half(ddx, dz, ch, h):
        b, rows = wb(ddx, dz, 0), g_rows(ch, h)
        return dot_nn(gt[0, rows, :], xbuf[b]) + dot_nn(gt[1, rows, :], xsib[b // 2])

    def put_dx(name, j, dy, ch, h, mine, dst, to):
        i, rows = j * 4 + dy, t_rows(ch, h, j)
        dxs[i, rows, :] = mine.astype(BF16)
        send(name, at(dxs, i, rows), dst, to)

    def put_dw(name, ddx, dz, ch, h, mine, dst, to):
        i, rows = ddx * 2 + dz, g_rows(ch, h)
        dws[i, rows, :] = mine.astype(BF16)
        send(name, at(dws, i, rows), dst, to)

    def s1(ch, j0, j1):
        for h, j, to in ((0, j0, yp), (1, j1, ym)):
            put_dx(("s1", h, j, ch), j, 2, ch, h, dx_half(j, 2, ch, h), at(ry_half, j * 2 + h, t_part(ch, j)), to)

    def s2n(ch, j0, j1):
        for h, j, dy, way, to in ((1, j1, 1, 0, yp), (0, j0, 3, 1, ym)):
            dst = at(ry_full, j * 2 + way, t_rows(ch, h, j))
            put_dx(("s2", j, way, h, ch), j, dy, ch, h, dx_half(j, dy, ch, h), dst, to)

    def s2d(ch, j0, j1):
        for h, j, dy, to in ((0, j0, 1, yp), (1, j1, 3, ym)):
            mine = dx_half(j, dy, ch, h)
            recv(("s1", h, j, ch), at(ry_half, j * 2 + h, t_part(ch, j)))
            mine = mine + value(ry_half, j * 2 + h, t_part(ch, j))
            put_dx(("s2", j, h, h, ch), j, dy, ch, h, mine, at(ry_full, j * 2 + h, t_rows(ch, h, j)), to)

    def s3(ch, j0, j1):
        for h, j in ((0, j0), (1, j1)):
            rows = t_rows(ch, h, j)
            mine = dx_half(j, 0, ch, h)
            for way in (0, 1):
                recv(("s2", j, way, h, ch), at(ry_full, j * 2 + way, rows))
                mine = mine + value(ry_full, j * 2 + way, rows)
            if j == 2:
                put_dx(("z1", h, ch), j, 0, ch, h, mine, at(rz_half, h, t_part(ch, j)), zp if h == 0 else zm)
            elif j == 0:
                for way in (0, 1):
                    for part in ((h,) if ch == 0 else (0, 1) if h == 0 else ()):
                        recv(("z2", way, part, ch), at(rz_full, way, t_rows(ch, part, 1)))
                    if ch == 1 and h == 1:
                        over_z = value(rz_full, way, slice(rows.start, MOST))
                        mine = jnp.concatenate([mine[:-LAST] + over_z, mine[-LAST:]], axis=0)
                    else:
                        mine = mine + value(rz_full, way, rows)
                dx_st[rows, :] = mine.astype(BF16)
                part_rows = pl.ds(rows.start, rows.stop - rows.start)
                store(dx_st.at[part_rows], dx_out.at[part_rows])
            else:
                way = 0 if j == 1 else 1
                if h == way:
                    recv(("z1", h, ch), at(rz_half, h, t_part(ch, j)))
                    mine = mine + value(rz_half, h, t_part(ch, j))
                put_dx(("z2", way, h, ch), j, 0, ch, h, mine, at(rz_full, way, rows), zp if j == 1 else zm)

    def t1(dz, ch):
        for h, to in ((0, xp), (1, xm)):
            put_dw(("t1", h, dz, ch), 2, dz, ch, h, dw_half(2, dz, ch, h), at(rx_half, dz * 2 + h, g_part(ch)), to)

    def t2n(dz, ch):
        for h, ddx, way, to in ((1, 1, 0, xp), (0, 3, 1, xm)):
            dst = at(rx_full, dz * 2 + way, g_rows(ch, h))
            put_dw(("t2", dz, way, h, ch), ddx, dz, ch, h, dw_half(ddx, dz, ch, h), dst, to)

    def t2d(dz, ch):
        for h, ddx, to in ((0, 1, xp), (1, 3, xm)):
            mine = dw_half(ddx, dz, ch, h)
            recv(("t1", h, dz, ch), at(rx_half, dz * 2 + h, g_part(ch)))
            mine = mine + value(rx_half, dz * 2 + h, g_part(ch))
            put_dw(("t2", dz, h, h, ch), ddx, dz, ch, h, mine, at(rx_full, dz * 2 + h, g_rows(ch, h)), to)

    def t3(dz, ch):
        for h in (0, 1):
            rows = g_rows(ch, h)
            mine = dw_half(0, dz, ch, h)
            for way in (0, 1):
                recv(("t2", dz, way, h, ch), at(rx_full, dz * 2 + way, rows))
                mine = mine + value(rx_full, dz * 2 + way, rows)
            if dz == 1:
                put_dw(("t3", h, ch), 0, 1, ch, h, mine, at(rzl, 0, rows), zlp)
            else:
                recv(("t3", h, ch), at(rzl, 0, rows))
                t_st[rows, :] = mine + value(rzl, 0, rows)
                for k in range(rows.start // HD, rows.stop // HD):
                    block = t_st[k * HD:(k + 1) * HD, :].T.astype(BF16)
                    if k < HEADS:
                        qg_st[:, k * HD:(k + 1) * HD] = block
                        store(qg_st.at[:, pl.ds(k * HD, HD)], qg_out.at[:, pl.ds(k * HD, HD)])
                    else:
                        kvg_st[...] = block
                        store(kvg_st, kvg_out)

    scale = HD ** -0.5

    def finish_role(i):
        rows = slice(i * HD, (i + 1) * HD)
        recv(("part", i), part_in.at[pl.ds(i * HD, HD)])
        total = part[role, rows, :] + part_in[rows, :].astype(F32)
        total = jnp.where(is_key, unrot(total, rows), total)
        gbuf[rows, FEAT:COLS] = total.astype(BF16)
        gt[0, FEAT:COLS, rows] = total.T.astype(BF16)

    for i in reversed(range(TOK // HD)):
        rows, n = slice(i * HD, (i + 1) * HD), (i + 1) * HD

        def head(h, carry, i=i, rows=rows, n=n):
            cols = pl.ds(pl.multiple_of(h * HD, HD), HD)
            q, grad = qbuf[rows, cols], og[rows, cols]
            k, v = kv[0, :n], kv[1, :n]
            scores = dot_nt(q, k)
            q_pos = lax.broadcasted_iota(jnp.int32, (HD, HD), 0)
            k_pos = lax.broadcasted_iota(jnp.int32, (HD, HD), 1)
            last = jnp.where(k_pos <= q_pos, scores[:, n - HD:], -jnp.inf)
            scores = last if i == 0 else jnp.concatenate([scores[:, :n - HD], last], axis=1)
            expo = jnp.exp2((scores - jnp.max(scores, axis=-1, keepdims=True)) * (scale * LOG2E))
            probs = expo * (1.0 / jnp.sum(expo, axis=-1, keepdims=True))
            dprobs = dot_nt(grad, v)
            delta = jnp.sum(probs * dprobs, axis=-1, keepdims=True)
            dscores = (probs * ((dprobs - delta) * scale)).astype(BF16)
            dq = unrot(dot_nn(dscores, k), rows)
            gbuf[rows, cols] = dq.astype(BF16)
            gt[0, cols, rows] = dq.T.astype(BF16)
            part[0, :n] += dot_tn(dscores, q)
            part[1, :n] += dot_tn(probs.astype(BF16), grad)
            return carry

        lax.fori_loop(0, HEADS, head, 0, unroll=4)
        part_low[rows, :] = part[1 - role, rows, :].astype(BF16)
        send(("part", i), part_low.at[pl.ds(i * HD, HD)], part_in.at[pl.ds(i * HD, HD)], mate)
        if i == 1:
            finish_role(2)
            s1(1, 2, 2)
            s2n(1, 2, 2)
            s1(1, 3, 1)

    send("gt_q", gt.at[0, pl.ds(0, FEAT)], gt.at[1, pl.ds(0, FEAT)], sib)
    q1()
    s2d(1, 2, 2)
    for i in range(8):
        recv(("xsib", i), xsib.at[i])
    recv("gt_q", gt.at[1, pl.ds(0, FEAT)])
    t1(1, 0)
    t2n(1, 0)
    finish_role(1)
    finish_role(0)
    send("gt_kv", gt.at[0, pl.ds(FEAT, HD)], gt.at[1, pl.ds(FEAT, HD)], sib)
    s1(0, 2, 2)
    q2()
    s2n(1, 3, 1)
    s3(1, 2, 2)
    t2d(1, 0)
    s2n(0, 2, 2)
    recv("gt_kv", gt.at[1, pl.ds(FEAT, HD)])
    t1(1, 1)
    s2d(1, 3, 1)
    s1(1, 1, 3)
    t2n(1, 1)
    s2n(1, 1, 3)
    s2d(0, 2, 2)
    s1(0, 3, 1)
    s3(1, 3, 1)
    t3(1, 0)
    t2d(1, 1)
    t1(0, 0)
    s2d(1, 1, 3)
    s2n(0, 3, 1)
    s3(0, 2, 2)
    s2d(0, 3, 1)
    t2n(0, 0)
    s1(0, 1, 3)
    s2n(0, 1, 3)
    t2d(0, 0)
    t1(0, 1)
    s3(1, 1, 3)
    s3(0, 3, 1)
    t3(1, 1)
    s2d(0, 1, 3)
    t2n(0, 1)
    q3()
    s1(1, 0, 0)
    s2n(1, 0, 0)
    s1(0, 0, 0)
    s2n(0, 0, 0)
    t2d(0, 1)
    s2d(1, 0, 0)
    t3(0, 0)
    s3(0, 1, 3)
    s2d(0, 0, 0)
    s3(1, 0, 0)
    t3(0, 1)
    s3(0, 0, 0)

    for copy in stores:
        copy.wait()
    for copy in pending[-N_SEND:]:
        copy.wait_send()
    assert len(names) <= N_SEMS


def hand_on(*refs):
    n = len(refs) // 3
    sources, targets, held = refs[:n], refs[n:2 * n], refs[2 * n:3 * n]
    sem_in, sem_out = refs[3 * n:]
    steps = []
    for i in range(n):
        size = held[i].shape[0] // 2
        for h in (0, 1):
            k, rows = 2 * i + h, pl.ds(h * size, size)
            steps.append((
                pltpu.make_async_copy(sources[i].at[rows], held[i].at[rows], sem_in.at[k]),
                pltpu.make_async_copy(held[i].at[rows], targets[i].at[rows], sem_out.at[k]),
            ))
    for into, _ in steps:
        into.start()
    for into, out in steps:
        into.wait()
        out.start()
    for _, out in steps:
        out.wait()


def body(tokens_in, out_grad, q_weight, kv_weight):
    cosine, sine = rope_tables(TOK, HD)
    anywhere = pl.BlockSpec(memory_space=pl.ANY)
    outs = (
        jax.ShapeDtypeStruct((TOK, FEAT), BF16),
        jax.ShapeDtypeStruct((FEAT, FEAT), BF16),
        jax.ShapeDtypeStruct((FEAT, HD), BF16),
    )
    results = pl.pallas_call(
        kernel,
        out_shape=outs,
        in_specs=[anywhere] * 6,
        out_specs=(anywhere,) * 3,
        scratch_shapes=[
            pltpu.VMEM((TOK, HD), F32),
            pltpu.VMEM((TOK, HD), F32),
            pltpu.VMEM((TOK, FEAT), BF16),
            pltpu.VMEM((FEAT, FEAT), BF16),
            pltpu.VMEM((FEAT, HD), BF16),
            pltpu.VMEM((COLS, FEAT), F32),
            pltpu.VMEM((16, TOK, FEAT), BF16),
            pltpu.VMEM((16, FEAT, COLS), BF16),
            pltpu.VMEM((8, TOK, FEAT), BF16),
            pltpu.VMEM((TOK, FEAT), BF16),
            pltpu.VMEM((TOK, COLS), F32),
            pltpu.VMEM((TOK, FEAT), BF16),
            pltpu.VMEM((2, TOK, HD), BF16),
            pltpu.VMEM((TOK, COLS), BF16),
            pltpu.VMEM((2, COLS, TOK), BF16),
            pltpu.VMEM((2, TOK, HD), F32),
            pltpu.VMEM((TOK, HD), BF16),
            pltpu.VMEM((TOK, HD), BF16),
            pltpu.VMEM((16, TOK, FEAT), BF16),
            pltpu.VMEM((8, TOK, FEAT), BF16),
            pltpu.VMEM((8, HT, FEAT), BF16),
            pltpu.VMEM((2, TOK, FEAT), BF16),
            pltpu.VMEM((2, HT, FEAT), BF16),
            pltpu.VMEM((2, 4, LAST, FEAT), BF16),
            pltpu.VMEM((2, 4, LAST // 2, FEAT), BF16),
            pltpu.VMEM((8, COLS, FEAT), BF16),
            pltpu.VMEM((4, COLS, FEAT), BF16),
            pltpu.VMEM((4, GC, FEAT), BF16),
            pltpu.VMEM((1, COLS, FEAT), BF16),
            pltpu.SemaphoreType.DMA((16,)),
            pltpu.SemaphoreType.DMA((N_SEND,)),
            pltpu.SemaphoreType.DMA((N_SEMS,)),
        ],
        compiler_params=pltpu.CompilerParams(
            collective_id=0, has_side_effects=True, vmem_limit_bytes=60 * 2**20
        ),
        name="attention_backward",
    )(tokens_in, out_grad, q_weight, kv_weight, jnp.asarray(cosine), jnp.asarray(sine))
    return pl.pallas_call(
        hand_on,
        out_shape=outs,
        in_specs=[anywhere] * 3,
        out_specs=(anywhere,) * 3,
        scratch_shapes=[pltpu.VMEM(o.shape, o.dtype) for o in outs] + [pltpu.SemaphoreType.DMA((6,))] * 2,
        name="hand_on",
    )(*results)


def solution(mesh):
    spec = P("dp", "tensor")
    return jax.shard_map(
        body, mesh=mesh, in_specs=(spec,) * 4, out_specs=(spec,) * 3, check_vma=False
    )
```
